32 devices in a mesh: blk: 16 (over z, y, core), shard: 2 (over x).
Axes of the slice: x: 2, y: 2, z: 4, core: 2. Of those that a mesh axis runs over, the one named last changes fastest.
Arguments:
- features: bfloat16 [2, 16384, 2048], P(None, ('blk', 'shard')), may hold values from -6 to 6
- weight: bfloat16 [2048, 2048], P(('blk', 'shard')), may hold values from -0.125 to 0.125
- bias: bfloat16 [2048], P(('blk', 'shard')), may hold values from -3 to 3
- cotangent: bfloat16 [2, 16384, 2048], P(None, ('blk', 'shard')), may hold values from -6 to 6
- neighbours: int32 [2, 16384, 16], P(None, ('blk', 'shard')), may hold values from -1 to 895, as said below
- live_count: int32 [2, 32], P(None, ('blk', 'shard')), may hold values from 128 to 512, as said below
Outputs:
- activated: bfloat16 [2, 16384, 2048], P(None, ('blk', 'shard'))
- feature_grad: bfloat16 [2, 16384, 2048], P(None, ('blk', 'shard'))
- weight_grad: float32 [2048, 2048], P(('blk', 'shard'))
- bias_grad: float32 [2048], P(('blk', 'shard'))
The draws below stay inside these ranges and needn't reach their ends.
Inputs may be any that keep to these rules, and one draw needn't show every extreme that they name: `neighbours`: for each slot, 16 entries in any order: -1 for an empty entry; c < the slot's live count for row c of the same device; 512 + s * 64 + r for row r of the device with shard index s in the same blk group; that plus 2 * 64 for the group before on the cycle (blk index minus 1, cyclic); that plus 2 * 2 * 64 for the group after. Slots at or beyond their device's live count hold only -1. `live_count`: devices are numbered blk-major. Each micro-batch has some device with all 512 slots live.
All inputs are finite; a program needn't handle non-finite values.
Results may differ from the reference program's by a relative error of at most 0.0059.
Values may be sent and summed in bfloat16 or wider, within the bound.
No kernel may reach another device: no remote copies, remote signals or barrier semaphores. Data moves between devices by JAX's collectives and lax.ppermute only.
A program may use at most 72 MiB of HBM per device.

```python
import jax
import jax.numpy as jnp
from jax import lax

D = 2048
NODES_DEV = 512
NBRS = 16
MB = 2
EDGE = 64
SPLIT = 2
NODES = 16384
N_BLK = 16
N_SHARD = 2
DEVICES = 32


def shared_counts(key):
    base_counts = jax.random.randint(key, (MB, DEVICES), NODES_DEV // 4, NODES_DEV + 1)
    column = jax.random.randint(jax.random.fold_in(key, 1), (MB, 1), 0, DEVICES)
    spots = jnp.arange(DEVICES)[None, :]
    return jnp.where(spots == column, NODES_DEV, base_counts).astype(jnp.int32)


def draw_live_count(key, part):
    return shared_counts(key)


def draw_neighbours(key, part):
    counts = shared_counts(key)
    key = jax.random.fold_in(key, 7)
    keys = jax.random.split(key, 4)
    shape = (MB, NODES, NBRS)
    device_of = jnp.arange(NODES) // NODES_DEV
    row_of = jnp.arange(NODES) % NODES_DEV
    own_count = counts[:, device_of]
    alive = (row_of[None, :] < own_count)[:, :, None]
    kinds = jax.random.randint(keys[0], shape, 0, 8)
    local_pick = jax.random.randint(keys[1], shape, 0, 1 << 20) % own_count[:, :, None]
    shard_pick = jax.random.randint(keys[2], shape, 0, SPLIT)
    row_pick = jax.random.randint(keys[3], shape, 0, EDGE)
    section = jnp.clip(kinds - 3, 0, 2)
    rim_code = NODES_DEV + section * (SPLIT * EDGE) + shard_pick * EDGE + row_pick
    result = jnp.where(kinds < 3, local_pick, jnp.where(kinds < 6, rim_code, -1))
    return jnp.where(alive, result, -1).astype(jnp.int32)


def raised(array, stream_key, source, target, parts, factor):
    owner, partner = [(jnp.arange(array.shape[dim]) // (array.shape[dim] // parts)).reshape([-1 if axis == dim else 1 for axis in range(array.ndim)]) for dim in (source, target)]
    chosen = jax.random.permutation(stream_key, parts)[partner]
    strong = (owner == chosen) | (owner == (partner + parts // 2) % parts)
    return jnp.where(strong, factor * array, array)


def levels(own_key, extent, cuts, least, top_value):
    loudness = 1.0
    for axis_at, parts in cuts:
        draws = jax.random.uniform(jax.random.fold_in(jax.random.fold_in(own_key, 6), axis_at), (parts,), jnp.float32, least / len(cuts), top_value / len(cuts))
        loudness = loudness * jnp.repeat(jnp.exp(draws), extent[axis_at] // parts).reshape((-1,) + (1,) * (len(extent) - 1 - axis_at))
    return loudness


def gaussian(key, dims, scale, reach, shards=(), kind=jnp.bfloat16):
    values = jax.random.normal(key, dims, jnp.float32) * scale
    if len(shards) > 0:
        values = levels(key, dims, shards, -0.22, 0.18) * values
    return jnp.clip(values, min=-reach, max=reach).astype(kind)


def noise_with(rng, dims, spread, bound, cuts, heavy, kind=jnp.bfloat16):
    drawn = spread * jax.random.normal(rng, dims, jnp.float32)
    if cuts:
        drawn = drawn * levels(rng, dims, cuts, -0.22, 0.18)
    return jnp.clip(raised(drawn, jax.random.fold_in(rng, 3), *heavy), -bound, bound).astype(kind)


def setup_inputs(seed: int = 0) -> dict:
    streams_of = jax.random.split(jax.random.key(seed), 7)
    features = noise_with(streams_of[0], (MB, NODES, D), 1.0, 6.0, ((1, 32),), (1, 2, 32, 2.75))
    weight = gaussian(streams_of[1], (D, D), D ** -0.5, 0.125, ((0, 32),))
    bias = gaussian(streams_of[2], (D,), 0.5, 3.0, ((0, 32),))
    cotangent = gaussian(streams_of[3], (MB, NODES, D), 1.0, 6.0, ((1, 32),))
    neighbours = draw_neighbours(jax.random.fold_in(streams_of[6], 71), 0)
    live_count = draw_live_count(jax.random.fold_in(streams_of[6], 71), 0)
    return dict(features=features, weight=weight, bias=bias, cotangent=cotangent, neighbours=neighbours, live_count=live_count)


@jax.custom_vjp
def low(v):
    return lax.optimization_barrier(v.astype(jnp.bfloat16)).astype(jnp.float32)

@jax.custom_vjp
def low_back(v):
    return v

def low_keep(v):
    return (low(v), None)

def low_pass(kept, grad):
    return (grad,)

def back_keep(v):
    return (v, None)

def back_low(kept, grad):
    return (low(grad),)
low.defvjp(low_keep, low_pass)
low_back.defvjp(back_keep, back_low)

def global_codes(neighbours):
    device_of = (jnp.arange(NODES, dtype=jnp.int32) // NODES_DEV)[None, :, None]
    group_of = device_of // N_SHARD
    shifted = neighbours - NODES_DEV
    span_rows = N_SHARD * EDGE
    section = shifted // span_rows
    shard_pick = shifted // EDGE % N_SHARD
    row_pick = shifted % EDGE
    offset = jnp.where(section == 1, -1, jnp.where(section == 2, 1, 0))
    target = (group_of + offset) % N_BLK
    far_slot = (target * N_SHARD + shard_pick) * NODES_DEV + row_pick
    near_slot = device_of * NODES_DEV + neighbours
    picked = jnp.where(neighbours < NODES_DEV, near_slot, far_slot)
    return jnp.where(neighbours < 0, -1, picked).astype(jnp.int32)

def aggregate(features_one, codes_one, alive_one):

    def one_device(packed):
        codes, alive, own = packed
        usable = (codes >= 0).astype(jnp.float32)
        lookup = jnp.where(codes >= 0, codes, 0).astype(jnp.int32)
        picked = jnp.take(features_one, lookup, axis=0)
        summed = lax.optimization_barrier(jnp.sum(picked * usable[:, :, None], axis=1))
        degree = lax.optimization_barrier(jnp.sum(usable, axis=1))
        weighting = alive / (degree + 1.0)
        return (summed + 2.0 * own) * weighting[:, None]
    packed = (codes_one.reshape(DEVICES, NODES_DEV, NBRS), alive_one.reshape(DEVICES, NODES_DEV), features_one.reshape(DEVICES, NODES_DEV, D))
    return lax.map(jax.checkpoint(one_device), packed).reshape(NODES, D)

def reference(features, weight, bias, cotangent, neighbours, live_count):
    codes_all = global_codes(neighbours)
    device_of = jnp.arange(NODES, dtype=jnp.int32) // NODES_DEV
    row_of = jnp.arange(NODES, dtype=jnp.int32) % NODES_DEV
    alive_all = (row_of[None, :] < live_count[:, device_of]).astype(jnp.float32)

    def forward(features_full, weight_full, bias_full):
        outputs = []
        for micro in range(MB):
            mixed = aggregate(features_full[micro], codes_all[micro], alive_all[micro])
            mixed_low = low(low_back(mixed))
            linear = low_back(jnp.dot(mixed_low, weight_full, precision=lax.Precision.HIGHEST) + bias_full)
            outputs.append(jax.nn.gelu(linear) * alive_all[micro][:, None])
        return jnp.stack(outputs)
    activated, pull = jax.vjp(forward, features.astype(jnp.float32), weight.astype(jnp.float32), bias.astype(jnp.float32))
    feature_grad, weight_grad, bias_grad = pull(cotangent.astype(jnp.float32))
    return (activated.astype(jnp.bfloat16), feature_grad.astype(jnp.bfloat16), weight_grad, bias_grad)
```

```python
import functools

import jax
import jax.numpy as jnp
import numpy as np
from jax import lax
from jax.experimental import pallas as pl
from jax.experimental.pallas import tpu as pltpu
from jax.sharding import PartitionSpec as P

BOTH = ("blk", "shard")
F32 = jnp.float32
BF16 = jnp.bfloat16
MIB = 1 << 20
GELU_A = 0.7978845608028654
GELU_B = 0.044715
ANY = pl.BlockSpec(memory_space=pl.ANY)
VMEM = pl.BlockSpec(memory_space=pltpu.VMEM)
SMEM = pl.BlockSpec(memory_space=pltpu.SMEM)

CHUNKS = (0.5, 0.5)
GATHER_ORDER = (("zxy", "zyx"), ("zxy", "zyx"))
REDUCE_ORDER = (("xyz", "yxz"), ("xyz", "yxz"))


def small_dot(a, b, contract=((1,), (0,))):
    return lax.dot_general(a, b, (contract, ((), ())), preferred_element_type=F32)


def count_kernel(rows, code_ref, code_t_ref, cnt_ref, cnt_t_ref):
    node_count, slots = code_ref.shape
    table = cnt_ref.shape[1]
    step = 32

    def by_node(i, carry):
        at = pl.ds(pl.multiple_of(i * step, step), step)
        codes = code_ref[at, :]
        column = lax.broadcasted_iota(jnp.int32, (step, table), 1)
        row = lax.broadcasted_iota(jnp.int32, (step, table), 0) + i * step
        total = jnp.where(column == row, 2.0, 0.0)
        for k in range(slots):
            total = total + jnp.where(column == codes[:, k : k + 1], 1.0, 0.0)
        cnt_ref[at, :] = total.astype(BF16)
        return carry

    def by_entry(i, carry):
        at = pl.ds(pl.multiple_of(i * step, step), step)
        row = lax.broadcasted_iota(jnp.int32, (step, node_count), 0) + i * step
        column = lax.broadcasted_iota(jnp.int32, (step, node_count), 1)
        total = jnp.where(column == row, 2.0, 0.0)
        for k in range(slots):
            total = total + jnp.where(row == code_t_ref[k : k + 1, :], 1.0, 0.0)
        cnt_t_ref[at, :] = total.astype(BF16)
        return carry

    lax.fori_loop(0, node_count // step, by_node, 0)
    lax.fori_loop(0, table // step, by_entry, 0)


def count_tables(codes, table):
    micro, node_count, slots = codes.shape
    return pl.pallas_call(
        functools.partial(count_kernel, node_count),
        grid=(micro,),
        in_specs=[
            pl.BlockSpec((None, node_count, slots), lambda m: (m, 0, 0)),
            pl.BlockSpec((None, slots, node_count), lambda m: (m, 0, 0)),
        ],
        out_specs=[
            pl.BlockSpec((None, node_count, table), lambda m: (m, 0, 0)),
            pl.BlockSpec((None, table, node_count), lambda m: (m, 0, 0)),
        ],
        out_shape=[
            jax.ShapeDtypeStruct((micro, node_count, table), BF16),
            jax.ShapeDtypeStruct((micro, table, node_count), BF16),
        ],
        compiler_params=pltpu.CompilerParams(vmem_limit_bytes=24 * MIB),
        name="count_tables",
    )(codes, jnp.swapaxes(codes, 1, 2))


def mix_kernel(cnt_ref, scale_ref, own_ref, *refs):
    piece_refs, (mixed_ref, mixed_t_ref, rim) = refs[:-3], refs[-3:]
    node_count = own_ref.shape[0]
    at = 0
    for piece in piece_refs:
        rim[at : at + piece.shape[0], :] = piece[...]
        at += piece.shape[0]
    total = small_dot(cnt_ref[:, :node_count], own_ref[...])
    total = total + small_dot(cnt_ref[:, node_count:], rim[...])
    scale = jnp.concatenate([scale_ref[...]] * (total.shape[1] // 128), axis=1)
    low = (total * scale).astype(BF16)
    mixed_ref[...] = low
    mixed_t_ref[...] = low.T


def mix(cnt, scale, features, pieces):
    micro, node_count, width = features.shape
    table = cnt.shape[2]
    wide = min(512, width)

    def along(rows):
        return pl.BlockSpec((None, rows, wide), lambda m, j: (m, 0, j))

    return pl.pallas_call(
        mix_kernel,
        grid=(micro, width // wide),
        in_specs=[
            pl.BlockSpec((None, node_count, table), lambda m, j: (m, 0, 0)),
            pl.BlockSpec((node_count, 128), lambda m, j: (m, 0)),
            along(node_count),
        ]
        + [along(piece.shape[1]) for piece in pieces],
        out_specs=[
            pl.BlockSpec((node_count, wide), lambda m, j: (m, j)),
            pl.BlockSpec((wide, node_count), lambda m, j: (j, m)),
        ],
        out_shape=[
            jax.ShapeDtypeStruct((micro * node_count, width), BF16),
            jax.ShapeDtypeStruct((width, micro * node_count), BF16),
        ],
        scratch_shapes=[pltpu.VMEM((table - node_count, wide), BF16)],
        compiler_params=pltpu.CompilerParams(vmem_limit_bytes=24 * MIB),
        name="mix",
    )(cnt, scale, features, *pieces)


def gelu_and_grad(linear, incoming, alive):
    square = linear * linear
    bend = jnp.tanh(linear * (GELU_A + (GELU_A * GELU_B) * square))
    share = 0.5 + 0.5 * bend
    value = linear * share
    slope = share + value * (1.0 - bend) * (GELU_A + (3.0 * GELU_A * GELU_B) * square)
    return (value * alive).astype(BF16), (incoming.astype(F32) * alive * slope).astype(BF16)


def layer_kernel(plan, *refs):
    start, size, first, last, piece_plan, tile, sub, block = plan
    n_pieces = len(piece_plan)
    (place_ref, slot_ref, half_ref, mixed, mixed_t, bias, cot, alive, scale) = refs[:9]
    pieces = refs[9 : 9 + n_pieces]
    rest = refs[9 + n_pieces :]
    acc_in = None
    if not first:
        acc_in, rest = rest[0], rest[2:]
    (act, send, keep, bias_grad, acc_out) = rest[:5]
    (wv, cv, av, lv, gv, linear, acc_a, acc_b, sem) = rest[5:]
    half = size // 2
    node_count = mixed.shape[0]
    width = mixed.shape[1]
    per = half // tile
    mine = half_ref[0]
    offsets = [
        pl.multiple_of(start + (1 - mine) * half, 128),
        pl.multiple_of(start + mine * half, 128),
    ]

    at = 0
    for ref, (side, count, rows) in zip(pieces, piece_plan):
        for i in range(count):
            into = pl.ds(pl.multiple_of(place_ref[at], rows), rows)
            pltpu.make_async_copy(ref.at[i], wv.at[side, into, :], sem.at[side]).start()
            at += 1
    cot_copies = []
    for side in range(2):
        copy = pltpu.make_async_copy(
            cot.at[:, pl.ds(offsets[side], half)], cv.at[side], sem.at[2 + side]
        )
        copy.start()
        cot_copies.append(copy)

    def where_is(t):
        return t // per, slice((t % per) * tile, (t % per + 1) * tile)

    def run_linear(t):
        side, cols = where_is(t)
        for m in range(0, node_count, sub):
            linear[t % 2, m : m + sub, :] = small_dot(mixed[m : m + sub, :], wv[side, :, cols])

    def run_gelu(t):
        side, cols = where_is(t)
        shift = bias[side, :, cols]
        total = jnp.zeros((8, tile), F32)
        rows = 64
        for m in range(0, node_count, rows):
            live = jnp.concatenate([alive[m : m + rows, :]] * (tile // 128), axis=1)
            value, grad = gelu_and_grad(
                linear[t % 2, m : m + rows, :] + shift, cv[side, m : m + rows, cols], live
            )
            av[side, m : m + rows, cols] = value
            lv[side, m : m + rows, cols] = grad
            total = total + jnp.sum(grad.astype(F32).reshape(rows // 8, 8, tile), axis=0)
        bias_grad[side, :, cols] = total

    def run_weight_grad(t):
        side, cols = where_is(t)
        for m in range(0, width, sub):
            part = small_dot(mixed_t[m : m + sub, :], lv[side, :, cols]).astype(BF16)
            for b in range(0, sub, block):
                into = pl.multiple_of(slot_ref[side, (m + b) // block] * block, block)
                gv[side, pl.ds(into, block), cols] = part[b : b + block]

    def all_weights(side):
        pltpu.make_async_copy(wv.at[side], wv.at[side], sem.at[side]).wait()

    outs = []
    all_weights(0)
    run_linear(0)
    for t in range(2 * per):
        if t + 1 == per:
            all_weights(1)
        if t + 1 < 2 * per:
            run_linear(t + 1)
        side = t // per
        if t % per == 0:
            cot_copies[side].wait()
        run_gelu(t)
        run_weight_grad(t)
        if (t + 1) % per == 0:
            for copy in (
                pltpu.make_async_copy(gv.at[side], (send, keep)[side], sem.at[4 + side]),
                pltpu.make_async_copy(
                    av.at[side], act.at[:, pl.ds(offsets[side], half)], sem.at[6 + side]
                ),
            ):
                copy.start()
                outs.append(copy)

    step = acc_b.shape[2]
    pending = [None, None]

    def fetch(i):
        return pltpu.make_async_copy(
            acc_in.at[:, i * step : (i + 1) * step], acc_a.at[i % 2], sem.at[8 + i % 2]
        )

    if not first:
        fetch(0).start()
    for i in range(width // step):
        if not first:
            fetch(i).wait()
            if i + 1 < width // step:
                fetch(i + 1).start()
        if pending[i % 2] is not None:
            pending[i % 2].wait()
        for m in range(0, node_count, sub):
            part = sum(
                small_dot(
                    lv[side, m : m + sub, :],
                    wv[side, i * step : (i + 1) * step, :],
                    ((1,), (1,)),
                )
                for side in range(2)
            )
            if not first:
                part = part + acc_a[i % 2, m : m + sub, :]
            if last:
                part = part * jnp.concatenate([scale[m : m + sub, :]] * (step // 128), axis=1)
            acc_b[i % 2, m : m + sub, :] = part.astype(acc_b.dtype)
        pending[i % 2] = pltpu.make_async_copy(
            acc_b.at[i % 2], acc_out.at[:, i * step : (i + 1) * step], sem.at[10 + i % 2]
        )
        pending[i % 2].start()
    for copy in pending + outs:
        if copy is not None:
            copy.wait()


def layer_chunk(start, size, last, place, slot, half, mixed, mixed_t, bias, cot, alive, scale, pieces, sides, before, block):
    node_count, width = mixed.shape
    first = before is None
    part = size // 2
    tile = min(256, part)
    step = min(256, width)
    sub = min(512, node_count)
    plan = (
        start,
        size,
        first,
        last,
        [(side, piece.shape[0], piece.shape[1]) for side, piece in zip(sides, pieces)],
        tile,
        sub,
        block,
    )
    acc_type = BF16 if last else F32
    operands = [place, slot, half, mixed, mixed_t, bias, cot, alive, scale, *pieces]
    specs = [SMEM, SMEM, SMEM, VMEM, VMEM, VMEM, ANY, VMEM, VMEM] + [ANY] * len(pieces)
    aliases = {}
    if not first:
        operands += list(before)
        specs += [ANY, ANY]
        aliases = {len(operands) - 1: 0}
    return pl.pallas_call(
        functools.partial(layer_kernel, plan),
        in_specs=specs,
        out_specs=[ANY, ANY, ANY, VMEM, ANY],
        out_shape=[
            jax.ShapeDtypeStruct((node_count, width), BF16),
            jax.ShapeDtypeStruct((width, part), BF16),
            jax.ShapeDtypeStruct((width, part), BF16),
            jax.ShapeDtypeStruct((2, 8, part), F32),
            jax.ShapeDtypeStruct((node_count, width), acc_type),
        ],
        scratch_shapes=[
            pltpu.VMEM((2, width, part), BF16),
            pltpu.VMEM((2, node_count, part), BF16),
            pltpu.VMEM((2, node_count, part), BF16),
            pltpu.VMEM((2, node_count, part), BF16),
            pltpu.VMEM((2, width, part), BF16),
            pltpu.VMEM((2, node_count, tile), F32),
            pltpu.VMEM((2, node_count, step), F32),
            pltpu.VMEM((2, node_count, step), acc_type),
            pltpu.SemaphoreType.DMA((12,)),
        ],
        input_output_aliases=aliases,
        compiler_params=pltpu.CompilerParams(vmem_limit_bytes=32 * MIB),
        name="layer_chunk",
    )(*operands)


def rim_grad_kernel(sizes, cnt_t_ref, grad_ref, *outs):
    node_count = grad_ref.shape[0]
    part = small_dot(cnt_t_ref[node_count:, :], grad_ref[...])
    at = 0
    for out, rows in zip(outs, sizes):
        out[...] = part[at : at + rows].astype(BF16)
        at += rows


def rim_grads(cnt_t, grad, sizes):
    micro, table, node_count = cnt_t.shape
    width = grad.shape[1]
    wide = min(512, width)
    return pl.pallas_call(
        functools.partial(rim_grad_kernel, sizes),
        grid=(micro, width // wide),
        in_specs=[
            pl.BlockSpec((None, table, node_count), lambda m, j: (m, 0, 0)),
            pl.BlockSpec((node_count, wide), lambda m, j: (m, j)),
        ],
        out_specs=[pl.BlockSpec((None, rows, wide), lambda m, j: (m, 0, j)) for rows in sizes],
        out_shape=[jax.ShapeDtypeStruct((micro, rows, width), BF16) for rows in sizes],
        compiler_params=pltpu.CompilerParams(vmem_limit_bytes=24 * MIB),
        name="rim_grads",
    )(cnt_t, grad)


def own_grad_kernel(cnt_t_ref, grad_ref, out_ref, head_ref):
    part = small_dot(cnt_t_ref[...], grad_ref[...])
    out_ref[...] = part.astype(BF16)
    head_ref[...] = part[: head_ref.shape[0]]


def own_grads(cnt_t, grad, rim_size):
    micro, _, node_count = cnt_t.shape
    width = grad.shape[1]
    wide = min(512, width)
    return pl.pallas_call(
        own_grad_kernel,
        grid=(micro, width // wide),
        in_specs=[
            pl.BlockSpec((None, node_count, node_count), lambda m, j: (m, 0, 0)),
            pl.BlockSpec((node_count, wide), lambda m, j: (m, j)),
        ],
        out_specs=[
            pl.BlockSpec((None, node_count, wide), lambda m, j: (m, 0, j)),
            pl.BlockSpec((None, rim_size, wide), lambda m, j: (m, 0, j)),
        ],
        out_shape=[
            jax.ShapeDtypeStruct((micro, node_count, width), BF16),
            jax.ShapeDtypeStruct((micro, rim_size, width), F32),
        ],
        compiler_params=pltpu.CompilerParams(vmem_limit_bytes=24 * MIB),
        name="own_grads",
    )(cnt_t, grad)


class Layout:
    def __init__(self, blks, shards):
        self.blks, self.shards = blks, shards
        self.tuned = shards == 2 and blks % 4 == 0
        self.sizes = {"z": blks // 4, "y": 2, "c": 2, "x": shards}

    def number(self, at):
        return ((at["z"] * 2 + at["y"]) * 2 + at["c"]) * self.shards + at["x"]

    def here(self):
        blk, shard = lax.axis_index("blk"), lax.axis_index("shard")
        return {"z": blk // 4, "y": blk // 2 % 2, "c": blk % 2, "x": shard}

    def spots(self):
        for z in range(self.sizes["z"]):
            for y in range(2):
                for c in range(2):
                    for x in range(self.shards):
                        yield {"z": z, "y": y, "c": c, "x": x}

    def shift(self, value, axes, by):
        pairs = []
        for spot in self.spots():
            axis = axes[spot["c"]]
            there = dict(spot)
            there[axis] = (spot[axis] + by) % self.sizes[axis]
            pairs.append((self.number(spot), self.number(there)))
        return lax.ppermute(value, BOTH, pairs)

    def swap(self, value):
        return self.shift(value, "cc", 1)


def from_shard(value, by):
    count = lax.axis_size("shard")
    return lax.ppermute(value, "shard", [(i, (i + by) % count) for i in range(count)])


def near_swap(value):
    count = lax.axis_size("blk")
    return lax.ppermute(value, "blk", [(i, i ^ 1) for i in range(count)])


def far_swap(value):
    count = lax.axis_size("blk")
    return lax.ppermute(value, "blk", [(i, (i + (1 if i % 2 else -1)) % count) for i in range(count)])


def gather_phases(layout, base, orders):
    steps = len(orders[0])
    current = base
    for step in range(steps):
        axes = (orders[0][step], orders[1][step])
        count = layout.sizes[axes[0]]
        got = [current] + [layout.shift(current, axes, k) for k in range(1, count)]
        if step == steps - 1:
            return got
        current = jnp.concatenate(got, axis=0)
    return [current]


def gathered_from(layout, order, bases):
    current = [{"c": b} for b in range(bases)]
    for axis in order:
        current = [dict(entry, **{axis: k}) for k in range(layout.sizes[axis]) for entry in current]
    return current


def gathered_numbers(layout, orders, bases, here, swapped):
    core = here["c"] ^ 1 if swapped else here["c"]
    tables = []
    for order in orders:
        entries = gathered_from(layout, order, bases)
        tables.append({axis: np.array([e[axis] for e in entries], np.int32) for axis in "zycx"})
    back = {axis: jnp.where(core == 0, tables[0][axis], tables[1][axis]) for axis in "zycx"}
    at = {axis: (here[axis] - back[axis]) % layout.sizes[axis] for axis in "zyx"}
    at["c"] = core ^ back["c"]
    return layout.number(at)


def slots_of(layout, orders, here, swapped):
    core = here["c"] ^ 1 if swapped else here["c"]
    number = np.arange(layout.blks * layout.shards)
    at = {
        "x": number % layout.shards,
        "c": number // layout.shards % 2,
        "y": number // layout.shards // 2 % 2,
        "z": number // layout.shards // 4,
    }
    results = []
    for order in orders:
        slot = 0
        for axis in order:
            count = layout.sizes[axis]
            ahead = (at[axis] - here[axis]) % count
            slot = slot * count + (ahead - 1) % count
        results.append(slot * 2 + (at["c"] ^ core))
    return jnp.where(core == 0, results[0], results[1]).astype(jnp.int32)


def reduce_phases(layout, parts, orders, kind):
    for step in range(len(orders[0])):
        axes = (orders[0][step], orders[1][step])
        count = layout.sizes[axes[0]]
        size = parts[0].shape[0] // count
        got = []
        for k in range(1, count):
            total = sum(part[(k - 1) * size : k * size].astype(F32) for part in parts)
            got.append(layout.shift(total.astype(kind), axes, k))
        parts = [part[(count - 1) * size :] for part in parts] + got
    return sum(part.astype(F32) for part in parts)


def per_device(layout, features, weight, bias, cotangent, neighbours, live_count):
    micro_count, node_count, width = features.shape
    shards = layout.shards
    devices = layout.blks * shards
    rim = node_count // 8
    own_rows = weight.shape[0]
    here = layout.here()
    core = here["c"]
    tuned = layout.tuned and own_rows % 16 == 0
    chunks = []
    at = 0
    for share in CHUNKS:
        chunks.append((at, int(width * share)))
        at += int(width * share)

    rim_own = features[:, :rim]
    rim_cross = [from_shard(rim_own, shards - k) for k in range(1, shards)]
    rim_far = far_swap(rim_own)

    if tuned:
        halves = [
            jnp.concatenate([weight[:, s + h * n // 2 : s + (h + 1) * n // 2] for s, n in chunks], axis=1)
            for h in range(2)
        ]
        ours = jnp.where(core == 0, halves[0], halves[1])
        theirs = layout.swap(jnp.where(core == 0, halves[1], halves[0]))
        base = jnp.stack([ours, theirs])

    rim_near = near_swap(jnp.concatenate([rim_own] + rim_cross, axis=1))
    rim_far_cross = [from_shard(rim_far, shards - k) for k in range(1, shards)]
    pieces = rim_cross + [rim_near, rim_far] + rim_far_cross
    table = node_count + sum(piece.shape[1] for piece in pieces)

    span = shards * rim
    shifted = neighbours - node_count
    section = shifted // span
    ahead = (shifted // rim % shards - here["x"]) % shards
    near_section = jnp.where(core == 0, 2, 1)
    base_slot = jnp.where(
        section == 0,
        node_count - rim,
        jnp.where(section == near_section, node_count + span - rim, node_count + 2 * span - rim),
    )
    slot = base_slot + ahead * rim + shifted % rim
    slot = jnp.where((section == 0) & (ahead == 0), shifted % rim, slot)
    codes = jnp.where(neighbours < node_count, neighbours, slot)
    degree = jnp.sum((neighbours >= 0).astype(F32), axis=2)
    alive = (jnp.arange(node_count, dtype=jnp.int32)[None, :] < live_count).astype(F32)
    weighting = alive / (degree + 1.0)
    total_nodes = micro_count * node_count
    alive_wide = jnp.broadcast_to(alive.reshape(total_nodes, 1), (total_nodes, 128))
    scale_wide = jnp.broadcast_to(weighting.reshape(total_nodes, 1), (total_nodes, 128))
    cnt, cnt_t = count_tables(codes, table)
    mixed, mixed_t = mix(cnt, scale_wide, features, pieces)

    if tuned:
        order = GATHER_ORDER[0]
        tiny = jnp.broadcast_to(jnp.pad(bias, (0, 128 - own_rows))[None, None, :], (1, 8, 128))
        tiny = jnp.concatenate([tiny, layout.swap(tiny)], axis=0)
        tiny = jnp.concatenate(gather_phases(layout, tiny, order), axis=0)[:, 0, :own_rows]
        owner = gathered_numbers(layout, order, 2, here, False)
        pick = (owner[None, :] == jnp.arange(devices)[:, None]).astype(F32)
        bias_full = jnp.dot(pick, tiny.astype(F32), precision=lax.Precision.HIGHEST).reshape(width)
    else:
        bias_full = lax.all_gather(bias, BOTH, axis=0, tiled=True).astype(F32)

    cot_rows = cotangent.reshape(total_nodes, width)
    before = None
    weight_grads = []
    bias_parts = []
    half_at = 0
    for j, (start, size) in enumerate(chunks):
        part = size // 2
        if tuned:
            order = GATHER_ORDER[j]
            mine = gather_phases(layout, base[:, :, half_at : half_at + part], order)
            other = [layout.swap(piece) for piece in mine]
            chunk_pieces = other + mine
            sides = [0] * len(other) + [1] * len(mine)
            place = jnp.concatenate(
                [gathered_numbers(layout, order, 2, here, flag) for flag in (True, False)]
            ) * own_rows
            slot_table = jnp.stack(
                [slots_of(layout, REDUCE_ORDER[j], here, flag) for flag in (True, False)]
            )
            block = own_rows
        else:
            whole = lax.all_gather(weight[:, start : start + size], BOTH, axis=0, tiled=True)
            low_half, high_half = whole[:, :part], whole[:, part:]
            chunk_pieces = [
                jnp.where(core == 0, high_half, low_half)[None],
                jnp.where(core == 0, low_half, high_half)[None],
            ]
            sides = [0, 1]
            place = jnp.zeros((2,), jnp.int32)
            block = 64
            slot_table = jnp.broadcast_to(jnp.arange(width // block, dtype=jnp.int32), (2, width // block))
        half_at += part
        pair = bias_full[start : start + size].reshape(2, 1, part)
        pair = jnp.where(core == 0, pair[::-1], pair)
        act, send, keep, bias_rows, acc = layer_chunk(
            start,
            size,
            j == len(chunks) - 1,
            place.astype(jnp.int32),
            slot_table.astype(jnp.int32),
            core.astype(jnp.int32).reshape(1),
            mixed,
            mixed_t,
            pair,
            cot_rows,
            alive_wide,
            scale_wide,
            chunk_pieces,
            sides,
            before,
            block,
        )
        before = (acc, act)
        bias_row = jnp.sum(bias_rows, axis=1)
        bias_parts.append(jnp.where(core == 0, bias_row[::-1], bias_row).reshape(size))
        if tuned:
            send = send.reshape(devices, own_rows, part)
            keep = keep.reshape(devices, own_rows, part)
            both = reduce_phases(layout, [keep, layout.swap(send)], REDUCE_ORDER[j], BF16)
            ours, theirs = both[0], layout.swap(both[1])
        else:
            ours = lax.psum_scatter(
                jnp.where(core == 0, keep, send), BOTH, scatter_dimension=0, tiled=True
            ).astype(F32)
            theirs = lax.psum_scatter(
                jnp.where(core == 0, send, keep), BOTH, scatter_dimension=0, tiled=True
            ).astype(F32)
        if tuned:
            low_half = jnp.where(core == 0, ours, theirs)
            high_half = jnp.where(core == 0, theirs, ours)
        else:
            low_half, high_half = ours, theirs
        weight_grads += [low_half, high_half]

    grad = acc
    sizes = [rim] * (shards - 1) + [span] + [rim] * shards
    parts = rim_grads(cnt_t, grad, sizes)
    cross, near, far = parts[: shards - 1], parts[shards - 1], parts[shards:]
    local, head = own_grads(cnt_t, grad, rim)
    near_back = near_swap(near).astype(F32)
    own_sum = near_back[:, :rim]
    far_sum = far[0].astype(F32)
    for k in range(1, shards):
        both = jnp.concatenate(
            [
                (cross[k - 1].astype(F32) + near_back[:, k * rim : (k + 1) * rim]).astype(BF16),
                far[k],
            ],
            axis=1,
        )
        both = from_shard(both, k).astype(F32)
        own_sum = own_sum + both[:, :rim]
        far_sum = far_sum + both[:, rim:]
    far_back = far_swap(far_sum.astype(BF16)).astype(F32)
    head = (head + own_sum + far_back).astype(BF16)
    feature_grad = lax.dynamic_update_slice(local, head, (0, 0, 0))

    bias_sum = jnp.concatenate(bias_parts)
    if tuned:
        order = REDUCE_ORDER[0]
        slot_table = slots_of(layout, order, here, False)
        pick = (slot_table[None, :] == jnp.arange(devices)[:, None]).astype(F32)
        tiny = jnp.dot(pick, bias_sum.reshape(devices, own_rows), precision=lax.Precision.HIGHEST)
        tiny = jnp.broadcast_to(
            jnp.pad(tiny, ((0, 0), (0, 128 - own_rows)))[:, None, :], (devices, 8, 128)
        )
        both = reduce_phases(layout, [tiny], order, F32)
        bias_out = (both[0] + layout.swap(both[1]))[0, :own_rows]
    else:
        bias_out = lax.psum_scatter(bias_sum, BOTH, scatter_dimension=0, tiled=True)

    return (
        before[1].reshape(features.shape),
        feature_grad,
        jnp.concatenate(weight_grads, axis=1),
        bias_out,
    )


def solution(mesh):
    layout = Layout(mesh.shape["blk"], mesh.shape["shard"])
    rows = P(None, BOTH, None)
    return jax.shard_map(
        functools.partial(per_device, layout),
        mesh=mesh,
        in_specs=(rows, P(BOTH, None), P(BOTH), rows, rows, P(None, BOTH)),
        out_specs=(rows, rows, P(BOTH, None), P(BOTH)),
        check_vma=False,
    )
```

```python
import functools

import jax
import jax.numpy as jnp
import numpy as np
from jax import lax
from jax.experimental import pallas as pl
from jax.experimental.pallas import tpu as pltpu
from jax.sharding import PartitionSpec as P

BOTH = ("blk", "shard")
F32 = jnp.float32
BF16 = jnp.bfloat16
MIB = 1 << 20
GELU_A = 0.7978845608028654
GELU_B = 0.044715
HBM = pl.BlockSpec(memory_space=pltpu.HBM)
VMEM = pl.BlockSpec(memory_space=pltpu.VMEM)
SMEM = pl.BlockSpec(memory_space=pltpu.SMEM)

CHUNKS = (0.5, 0.5)
GATHER_ORDER = ("hlxy", "hlyx")
REDUCE_ORDER = (("xylh", "yxlh"), ("xylh", "yxlh"))


def cost(us):
    return pl.CostEstimate(flops=int(us * 1.1e9), bytes_accessed=0, transcendentals=0)


def held(array, space):
    return pltpu.with_memory_space_constraint(array, space)


def small_dot(a, b, contract=((1,), (0,))):
    return lax.dot_general(a, b, (contract, ((), ())), preferred_element_type=F32)


def count_kernel(code_ref, cnt_ref, cnt_t_ref):
    node_count, slots = code_ref.shape
    table = cnt_ref.shape[1]
    step = 64
    kind = jnp.int16

    def some_nodes(i, carry):
        at = pl.ds(pl.multiple_of(i * step, step), step)
        codes = code_ref[at, :].astype(kind)
        column = lax.broadcasted_iota(kind, (step, table), 1)
        row = lax.broadcasted_iota(kind, (step, table), 0) + (i * step).astype(kind)
        total = jnp.where(column == row, BF16(2), BF16(0))
        for k in range(slots):
            total = total + jnp.where(column == codes[:, k : k + 1], BF16(1), BF16(0))
        cnt_ref[at, :] = total
        return carry

    lax.fori_loop(0, node_count // step, some_nodes, 0)
    cnt_t_ref[...] = cnt_ref[...].T


def count_tables(codes, table):
    micro, node_count, slots = codes.shape
    return pl.pallas_call(
        count_kernel,
        grid=(micro,),
        in_specs=[pl.BlockSpec((None, node_count, slots), lambda m: (m, 0, 0))],
        out_specs=[
            pl.BlockSpec((None, node_count, table), lambda m: (m, 0, 0)),
            pl.BlockSpec((None, table, node_count), lambda m: (m, 0, 0)),
        ],
        out_shape=[
            jax.ShapeDtypeStruct((micro, node_count, table), BF16),
            jax.ShapeDtypeStruct((micro, table, node_count), BF16),
        ],
        compiler_params=pltpu.CompilerParams(vmem_limit_bytes=24 * MIB),
        cost_estimate=cost(6),
        name="count_tables",
    )(codes)


def mix_kernel(counts, cnt_ref, scale_ref, own_ref, *refs):
    piece_refs, (mixed_ref, mixed_t_ref, token_ref, rim) = refs[:-4], refs[-4:]
    node_count = own_ref.shape[0]
    for micro, count in enumerate(counts):
        first = sum(counts[:micro])

        @pl.when(pl.program_id(0) == micro)
        def _():
            at = 0
            for piece in piece_refs[first : first + count]:
                rim[at : at + piece.shape[0], :] = piece[...]
                at += piece.shape[0]

    total = small_dot(cnt_ref[:, :node_count], own_ref[...])
    total = total + small_dot(cnt_ref[:, node_count:], rim[...])
    scale = jnp.concatenate([scale_ref[...]] * (total.shape[1] // 128), axis=1)
    low = (total * scale).astype(BF16)
    mixed_ref[...] = low
    mixed_t_ref[...] = low.T
    token_ref[...] = jnp.zeros_like(token_ref)


def mix(cnt, scale, features, pieces):
    micro, node_count, width = features.shape
    table = cnt.shape[2]
    wide = min(512, width)

    def rows_of(piece, which):
        return pl.BlockSpec(
            (piece.shape[0], wide), lambda m, j: (0, jnp.where(m == which, j, (micro - 1 - m) * 0))
        )

    return pl.pallas_call(
        functools.partial(mix_kernel, [len(group) for group in pieces]),
        grid=(micro, width // wide),
        in_specs=[
            pl.BlockSpec((None, node_count, table), lambda m, j: (m, 0, 0)),
            pl.BlockSpec((node_count, 128), lambda m, j: (m, 0)),
            pl.BlockSpec((None, node_count, wide), lambda m, j: (m, 0, j)),
        ]
        + [rows_of(piece, which) for which in range(micro) for piece in pieces[which]],
        out_specs=[
            pl.BlockSpec((node_count, wide), lambda m, j: (m, j)),
            pl.BlockSpec((wide, node_count), lambda m, j: (j, m)),
            pl.BlockSpec((8, 128), lambda m, j: (0, 0)),
        ],
        out_shape=[
            pltpu.VMEM((micro * node_count, width), BF16),
            pltpu.VMEM((width, micro * node_count), BF16),
            jax.ShapeDtypeStruct((8, 128), F32),
        ],
        scratch_shapes=[pltpu.VMEM((table - node_count, wide), BF16)],
        compiler_params=pltpu.CompilerParams(vmem_limit_bytes=24 * MIB),
        cost_estimate=cost(6),
        name="mix",
    )(cnt, scale, features, *[piece for group in pieces for piece in group])


def gelu_and_grad(linear, incoming, alive):
    square = linear * linear
    bend = jnp.tanh(linear * (GELU_A + (GELU_A * GELU_B) * square))
    share = 0.5 + 0.5 * bend
    value = linear * share
    slope = share + value * (1.0 - bend) * (GELU_A + (3.0 * GELU_A * GELU_B) * square)
    return (value * alive).astype(BF16), (incoming.astype(F32) * alive * slope).astype(BF16)


def half_kernel(plan, *refs):
    start, half, side, first, tail, keeps, whole, blocks, bias_blocks, inner, rows, tile, sub, block = plan
    refs = list(refs)
    place_ref, chip_ref, slot_ref, half_ref, _, mixed, mixed_t, cot, alive = refs[:9]
    del refs[:9]
    n_pieces = 1 if whole else len(blocks)
    pieces = refs[:n_pieces]
    del refs[:n_pieces]
    bias_pieces = refs[: len(bias_blocks)]
    del refs[: len(bias_blocks)]
    bias = None if bias_blocks else refs.pop(0)
    bias_sums_in = None
    if not first:
        bias_sums_in = refs[0]
        del refs[:2]
    act, out, bias_sums, grad_out, wv = refs[:5]
    del refs[:5]
    bias_out = refs.pop(0) if bias_blocks else None
    cv, av, gv, linear, bias_raw, sem = refs
    node_count, width = mixed.shape
    tiles = half // tile
    mine = half_ref[0]
    holder = mine if side else 1 - mine
    offset = pl.multiple_of(start + holder * half, 128)

    def columns(t):
        return slice(t * tile, (t + 1) * tile)

    for t in range(tiles):
        at = 0
        if whole:
            part = pl.ds(pl.multiple_of(holder * half + t * tile, 128), tile)
            pltpu.make_async_copy(pieces[0].at[:, part], wv.at[:, columns(t)], sem.at[t]).start()
        for ref, count in zip(pieces, blocks):
            for i in range(count):
                for k in range(inner):
                    into = pl.ds(pl.multiple_of(place_ref[side, at], rows), rows)
                    pltpu.make_async_copy(
                        ref.at[i, k * rows : (k + 1) * rows, columns(t)],
                        wv.at[into, columns(t)],
                        sem.at[t],
                    ).start()
                    at += 1
        if t == 0:
            seen = 0
            for ref, count in zip(bias_pieces, bias_blocks):
                for i in range(count):
                    pltpu.make_async_copy(
                        ref.at[i, inner * rows : inner * rows + 16, 0:128],
                        bias_raw.at[chip_ref[seen]],
                        sem.at[tiles + 2],
                    ).start()
                    seen += 1
            cot_copy = pltpu.make_async_copy(cot.at[:, pl.ds(offset, half)], cv, sem.at[tiles])
            cot_copy.start()

    if first:
        bias_sums[...] = jnp.zeros_like(bias_sums)
    else:
        bias_sums[...] = bias_sums_in[...]
    if bias_blocks:
        pltpu.make_async_copy(bias_raw, bias_raw, sem.at[tiles + 2]).wait()
        for chip in range(bias_raw.shape[0] // 2):
            pair = bias_raw[2 * chip].astype(F32) + bias_raw[2 * chip + 1].astype(F32)
            bias_out[2 * chip] = jnp.where(mine == 0, pair[:8], pair[8:])
            bias_out[2 * chip + 1] = jnp.where(mine == 0, pair[8:], pair[:8])
        bias = bias_out

    def run_linear(t):
        pltpu.make_async_copy(wv.at[:, columns(t)], wv.at[:, columns(t)], sem.at[t]).wait()
        for m in range(0, node_count, sub):
            linear[t % 2, m : m + sub, :] = small_dot(mixed[m : m + sub, :], wv[:, columns(t)])

    def run_gelu(t):
        group = offset // 128 + t * (tile // 128)
        shift = jnp.concatenate([bias[group + k] for k in range(tile // 128)], axis=1)[:1]
        total = jnp.zeros((8, tile), F32)
        step = 64
        for m in range(0, node_count, step):
            live = jnp.concatenate([alive[m : m + step, :]] * (tile // 128), axis=1)
            value, grad = gelu_and_grad(
                linear[t % 2, m : m + step, :] + shift, cv[m : m + step, columns(t)], live
            )
            av[m : m + step, columns(t)] = value
            grad_out[m : m + step, columns(t)] = grad
            total = total + jnp.sum(grad.astype(F32).reshape(step // 8, 8, tile), axis=0)
        for k in range(tile // 128):
            bias_sums[group + k] = total[:, k * 128 : (k + 1) * 128]

    def run_weight_grad(t):
        for m in range(0, width, sub):
            part = small_dot(mixed_t[m : m + sub, :], grad_out[:, columns(t)]).astype(BF16)
            for b in range(0, sub, block):
                into = pl.multiple_of(slot_ref[side, (m + b) // block], 16)
                gv[pl.ds(into, block), columns(t)] = part[b : b + block]

    run_linear(0)
    cot_copy.wait()
    for t in range(tiles):
        if t + 1 < tiles:
            run_linear(t + 1)
        run_gelu(t)
        run_weight_grad(t)
    act_copy = pltpu.make_async_copy(av, act.at[:, pl.ds(offset, half)], sem.at[tiles + 1])
    act_copy.start()
    if tail:
        for pair in range(width // block // 2):
            chip = pair // 2
            base = slot_ref[side, chip * 4 + pair % 2] - holder * block
            if keeps:
                both = jnp.concatenate(
                    [bias_sums[2 * chip + holder], bias_sums[2 * chip + 1 - holder]], axis=0
                )
                both = jnp.concatenate([both, jnp.zeros((16, half - 128), F32)], axis=1)
            else:
                both = jnp.zeros((16, half), F32)
            gv[pl.ds(pl.multiple_of(base + 2 * block, 16), 16), :] = both.astype(BF16)
    out_copy = pltpu.make_async_copy(gv, out, sem.at[tiles])
    out_copy.start()
    act_copy.wait()
    out_copy.wait()


def layer_half(
    start, half, side, tail, tables, token, mixed, mixed_t, bias, cot, alive, pieces, bias_pieces, rows, before, block
):
    node_count, width = mixed.shape
    first = before is None
    tile = min(256, half)
    sub = min(512, node_count)
    groups = width // 128
    out_rows = width + 16 * (width // block // 2) if tail else width
    plan = (
        start,
        half,
        side,
        first,
        tail,
        tail and side == 1,
        pieces[0].ndim == 2,
        [piece.shape[0] for piece in pieces if piece.ndim == 3],
        [piece.shape[0] for piece in bias_pieces],
        2,
        rows,
        tile,
        sub,
        block,
    )
    operands = [*tables, token]
    operands += [held(array, pltpu.VMEM) for array in (mixed, mixed_t)]
    operands += [held(cot, pltpu.HBM), alive]
    operands += [held(array, pltpu.HBM) for array in (*pieces, *bias_pieces)]
    specs = [SMEM] * 4 + [HBM, VMEM, VMEM, HBM, VMEM] + [HBM] * (len(pieces) + len(bias_pieces))
    if not bias_pieces:
        operands.append(bias)
        specs.append(VMEM)
    aliases = {}
    if not first:
        operands += list(before)
        specs += [VMEM, HBM]
        aliases = {len(operands) - 1: 0}
    out_specs = [HBM, HBM, VMEM, VMEM, VMEM]
    out_shape = [
        pltpu.HBM((node_count, width), BF16),
        pltpu.HBM((out_rows, half), BF16),
        jax.ShapeDtypeStruct((groups, 8, 128), F32),
        pltpu.VMEM((node_count, half), BF16),
        pltpu.VMEM((width, half), BF16),
    ]
    if bias_pieces:
        out_specs.append(VMEM)
        out_shape.append(jax.ShapeDtypeStruct((groups, 8, 128), F32))
    return pl.pallas_call(
        functools.partial(half_kernel, plan),
        in_specs=specs,
        out_specs=out_specs,
        out_shape=out_shape,
        scratch_shapes=[
            pltpu.VMEM((node_count, half), BF16),
            pltpu.VMEM((node_count, half), BF16),
            pltpu.VMEM((out_rows, half), BF16),
            pltpu.VMEM((2, node_count, tile), F32),
            pltpu.VMEM((groups, 16, 128), BF16),
            pltpu.SemaphoreType.DMA((half // tile + 3,)),
        ],
        input_output_aliases=aliases,
        compiler_params=pltpu.CompilerParams(vmem_limit_bytes=16 * MIB),
        cost_estimate=cost(8),
        name="layer_half",
    )(*operands)


def mixed_grad_kernel(count, scale, *refs):
    grads, weights, out = refs[:count], refs[count : 2 * count], refs[2 * count]
    node_count, width = out.shape
    tile = min(256, width)
    sub = min(512, node_count)
    for d in range(0, width, tile):
        for m in range(0, node_count, sub):
            part = sum(
                small_dot(grad[m : m + sub, :], weight[d : d + tile, :], ((1,), (1,)))
                for grad, weight in zip(grads, weights)
            )
            part = part * jnp.concatenate([scale[m : m + sub, :]] * (tile // 128), axis=1)
            out[m : m + sub, d : d + tile] = part.astype(BF16)


def mixed_grad(scale, grads, weights):
    node_count, width = grads[0].shape[0], weights[0].shape[0]
    return pl.pallas_call(
        functools.partial(mixed_grad_kernel, len(grads)),
        in_specs=[VMEM] * (1 + 2 * len(grads)),
        out_specs=VMEM,
        out_shape=jax.ShapeDtypeStruct((node_count, width), BF16),
        compiler_params=pltpu.CompilerParams(vmem_limit_bytes=16 * MIB),
        cost_estimate=cost(10),
        name="mixed_grad",
    )(scale, *[held(array, pltpu.VMEM) for array in (*grads, *weights)])


def rim_grad_kernel(sizes, cnt_t_ref, grad_ref, *outs):
    node_count = grad_ref.shape[0]
    part = small_dot(cnt_t_ref[node_count:, :], grad_ref[...])
    at = 0
    for out, rows in zip(outs, sizes):
        out[...] = part[at : at + rows].astype(BF16)
        at += rows


def rim_grads(cnt_t, grad, sizes):
    micro, table, node_count = cnt_t.shape
    width = grad.shape[1]
    wide = min(512, width)
    return pl.pallas_call(
        functools.partial(rim_grad_kernel, sizes),
        grid=(micro, width // wide),
        in_specs=[
            pl.BlockSpec((None, table, node_count), lambda m, j: (m, 0, 0)),
            pl.BlockSpec((node_count, wide), lambda m, j: (m, j)),
        ],
        out_specs=[pl.BlockSpec((None, rows, wide), lambda m, j: (m, 0, j)) for rows in sizes],
        out_shape=[jax.ShapeDtypeStruct((micro, rows, width), BF16) for rows in sizes],
        compiler_params=pltpu.CompilerParams(vmem_limit_bytes=24 * MIB),
        cost_estimate=cost(3),
        name="rim_grads",
    )(cnt_t, grad)


def own_grad_kernel(cnt_t_ref, grad_ref, out_ref, head_ref):
    part = small_dot(cnt_t_ref[...], grad_ref[...])
    out_ref[...] = part.astype(BF16)
    head_ref[...] = part[: head_ref.shape[0]]


def own_grads(cnt_t, grad, rim_size):
    micro, _, node_count = cnt_t.shape
    width = grad.shape[1]
    wide = min(512, width)
    return pl.pallas_call(
        own_grad_kernel,
        grid=(micro, width // wide),
        in_specs=[
            pl.BlockSpec((None, node_count, node_count), lambda m, j: (m, 0, 0)),
            pl.BlockSpec((node_count, wide), lambda m, j: (m, j)),
        ],
        out_specs=[
            pl.BlockSpec((None, node_count, wide), lambda m, j: (m, 0, j)),
            pl.BlockSpec((None, rim_size, wide), lambda m, j: (m, 0, j)),
        ],
        out_shape=[
            jax.ShapeDtypeStruct((micro, node_count, width), BF16),
            jax.ShapeDtypeStruct((micro, rim_size, width), F32),
        ],
        compiler_params=pltpu.CompilerParams(vmem_limit_bytes=24 * MIB),
        cost_estimate=cost(4),
        name="own_grads",
    )(cnt_t, grad)


class Layout:
    def __init__(self, blks, shards):
        self.blks, self.shards = blks, shards
        self.tuned = shards == 2 and blks == 16
        self.sizes = {"h": blks // 8, "l": 2, "y": 2, "c": 2, "x": shards}

    def number(self, at):
        blk = ((at["h"] * 2 + at["l"]) * 2 + at["y"]) * 2 + at["c"]
        return blk * self.shards + at["x"]

    def place(self, blk, shard):
        return {"h": blk // 8, "l": blk // 4 % 2, "y": blk // 2 % 2, "c": blk % 2, "x": shard}

    def here(self):
        return self.place(lax.axis_index("blk"), lax.axis_index("shard"))

    def spots(self):
        for number in range(self.blks * self.shards):
            yield self.place(number // self.shards, number % self.shards)

    def shift(self, value, axes, by):
        pairs = []
        for spot in self.spots():
            axis = axes[spot["c"]]
            there = dict(spot)
            there[axis] = (spot[axis] + by) % self.sizes[axis]
            pairs.append((self.number(spot), self.number(there)))
        return lax.ppermute(value, BOTH, pairs)

    def swap(self, value):
        return self.shift(value, "cc", 1)


def from_shard(value, by):
    count = lax.axis_size("shard")
    return lax.ppermute(value, "shard", [(i, (i + by) % count) for i in range(count)])


def near_swap(value):
    count = lax.axis_size("blk")
    return lax.ppermute(value, "blk", [(i, i ^ 1) for i in range(count)])


def far_swap(value):
    count = lax.axis_size("blk")
    return lax.ppermute(value, "blk", [(i, (i + (1 if i % 2 else -1)) % count) for i in range(count)])


def tie(value, *others):
    return lax.optimization_barrier((value, others))[0]


def gather_step(layout, current, orders, step):
    axes = (orders[0][step], orders[1][step])
    return [current] + [
        layout.shift(current, axes, k) for k in range(1, layout.sizes[axes[0]])
    ]


def reduce_step(layout, parts, orders, step):
    size = parts[0].shape[0] // layout.sizes[orders[0][step]]
    return [
        sum(part[k * size : (k + 1) * size].astype(F32) for part in parts).astype(BF16)
        for k in range(layout.sizes[orders[0][step]] - 1)
    ]


def reduce_send(layout, parts, sums, orders, step):
    axes = (orders[0][step], orders[1][step])
    got = [layout.shift(total, axes, k + 1) for k, total in enumerate(sums)]
    return [part[part.shape[0] - sums[0].shape[0] :] for part in parts] + got


def gathered_from(layout, order, bases):
    current = [{"c": b} for b in range(bases)]
    for axis in order:
        current = [dict(entry, **{axis: k}) for k in range(layout.sizes[axis]) for entry in current]
    return current


def gathered_numbers(layout, orders, bases, here, swapped):
    core = here["c"] ^ 1 if swapped else here["c"]
    tables = []
    for order in orders:
        entries = gathered_from(layout, order, bases)
        tables.append({axis: np.array([e[axis] for e in entries], np.int32) for axis in "hlycx"})
    back = {axis: jnp.where(core == 0, tables[0][axis], tables[1][axis]) for axis in "hlycx"}
    at = {axis: (here[axis] - back[axis]) % layout.sizes[axis] for axis in "hlyx"}
    at["c"] = core ^ back["c"]
    return layout.number(at)


def slots_of(layout, orders, here, swapped):
    core = here["c"] ^ 1 if swapped else here["c"]
    number = np.arange(layout.blks * layout.shards)
    at = layout.place(number // layout.shards, number % layout.shards)
    results = []
    for order in orders:
        slot = 0
        for axis in order:
            count = layout.sizes[axis]
            ahead = (at[axis] - here[axis]) % count
            slot = slot * count + (ahead - 1) % count
        results.append(slot * 2 + (at["c"] ^ core))
    return jnp.where(core == 0, results[0], results[1]).astype(jnp.int32)


def per_device(layout, features, weight, bias, cotangent, neighbours, live_count):
    micro_count, node_count, width = features.shape
    shards = layout.shards
    devices = layout.blks * shards
    rim = node_count // 8
    span = shards * rim
    own_rows = weight.shape[0]
    here = layout.here()
    core = here["c"]
    tuned = layout.tuned and own_rows * shards == 128
    chunks = []
    at = 0
    for share in CHUNKS:
        chunks.append((at, int(width * share)))
        at += int(width * share)
    back_a, back_b = REDUCE_ORDER

    rim_own = [features[m, :rim] for m in range(2)]
    far_0 = [far_swap(rim_own[0])]
    cross_1 = [from_shard(rim_own[1], shards - k) for k in range(1, shards)]
    if tuned:
        block = rows = own_rows
        numbers = [gathered_numbers(layout, GATHER_ORDER, 2, here, flag) for flag in (True, False)]
        place = jnp.stack(numbers) * own_rows
        chip = (numbers[1] // 4 * 2 + numbers[1] % 2)[::2]
        slots = [
            jnp.stack([slots_of(layout, order, here, flag) for flag in (True, False)])
            for order in REDUCE_ORDER
        ]
        slots = [
            slot // 2 * (2 * block + extra) + slot % 2 * block
            for slot, extra in zip(slots, (0, 16))
        ]
        halves = [
            jnp.concatenate([weight[:, s + h * n // 2 : s + (h + 1) * n // 2] for s, n in chunks], axis=1)
            for h in range(2)
        ]
        lane = jnp.where(
            here["x"] == 0, jnp.pad(bias, (0, 128 - own_rows)), jnp.pad(bias, (128 - own_rows, 0))
        )
        bias_block = jnp.broadcast_to(jnp.pad(lane, (0, width // 2 - 128))[None], (8, width // 2))
        ours = jnp.where(core == 0, halves[0], halves[1])
        theirs = layout.swap(
            jnp.concatenate([jnp.where(core == 0, halves[1], halves[0]), bias_block], axis=0)
        )
        half = chunks[0][1] // 2
        bases = [
            jnp.concatenate(
                [
                    ours[:, :half],
                    theirs[:own_rows, :half],
                    bias_block[:, :half],
                    theirs[own_rows:, :half],
                ],
                axis=0,
            )[None],
            jnp.concatenate([ours[:, half:], theirs[:own_rows, half:]], axis=0)[None],
        ]
        got_a = gather_step(layout, bases[0], GATHER_ORDER, 0)
    else:
        block = rows = 64
        place = jnp.zeros((2, 1), jnp.int32)
        chip = jnp.zeros((2,), jnp.int32)
        slots = [
            jnp.broadcast_to(jnp.arange(0, width, block, dtype=jnp.int32), (2, width // block))
        ] * 2
        theirs = weight
        wholes = [
            lax.all_gather(weight[:, start : start + size], BOTH, axis=0, tiled=True)
            for start, size in chunks
        ]
    tables = [array.astype(jnp.int32) for array in (place, chip, *slots, core.reshape(1))]
    neighbours, tables = tie((neighbours, tables), theirs)

    table = node_count + (3 * shards - 1) * rim
    shifted = neighbours - node_count
    section = shifted // span
    ahead = (shifted // rim % shards - here["x"]) % shards
    near_section = jnp.where(core == 0, 2, 1)
    base_slot = jnp.where(
        section == 0,
        node_count - rim,
        jnp.where(section == near_section, node_count + span - rim, node_count + 2 * span - rim),
    )
    slot = base_slot + ahead * rim + shifted % rim
    slot = jnp.where((section == 0) & (ahead == 0), shifted % rim, slot)
    codes = jnp.where(neighbours < node_count, neighbours, slot)
    degree = jnp.sum((neighbours >= 0).astype(F32), axis=2)
    alive = (jnp.arange(node_count, dtype=jnp.int32)[None, :] < live_count).astype(F32)
    weighting = alive / (degree + 1.0)
    total_nodes = micro_count * node_count
    alive_wide = jnp.broadcast_to(alive.reshape(total_nodes, 1), (total_nodes, 128))
    scale_wide = jnp.broadcast_to(weighting.reshape(total_nodes, 1), (total_nodes, 128))
    cnt, cnt_t = count_tables(codes, table)

    if tuned:
        current = jnp.concatenate(got_a)
        current, far_0, cross_1, cnt, cnt_t, alive_wide, scale_wide, base_b = lax.optimization_barrier(
            (current, far_0, cross_1, cnt, cnt_t, alive_wide, scale_wide, bases[1])
        )
        got_a = gather_step(layout, current, GATHER_ORDER, 1)
    hop = jnp.concatenate([rim_own[0], far_0[0]])
    hop = [from_shard(hop, shards - k) for k in range(1, shards)]
    cross_0 = [both[:rim] for both in hop]
    far_0 = far_0 + [both[rim:] for both in hop]
    group_1 = jnp.concatenate([rim_own[1]] + cross_1)
    far_1 = [far_swap(group_1)]
    near_1 = near_swap(group_1)

    if tuned:
        current = jnp.concatenate(got_a)
        current, cross_0, far_0, far_1, near_1, base_b = lax.optimization_barrier(
            (current, cross_0, far_0, far_1, near_1, base_b)
        )
        got_a = gather_step(layout, current, GATHER_ORDER, 2)
        got_b = gather_step(layout, base_b, GATHER_ORDER, 0)
    near_0 = near_swap(jnp.concatenate([rim_own[0]] + cross_0))

    if tuned:
        last_a, current = jnp.concatenate(got_a), jnp.concatenate(got_b)
        last_a, current, near_0 = lax.optimization_barrier((last_a, current, near_0))
        got_a = gather_step(layout, last_a, GATHER_ORDER, 3)
        others_a = [layout.swap(last_a)]
        got_b = gather_step(layout, current, GATHER_ORDER, 1)
    mixed, mixed_t, token = mix(
        cnt, scale_wide, features, [cross_0 + [near_0] + far_0, cross_1 + [near_1] + far_1]
    )

    if tuned:
        current = jnp.concatenate(got_b)
        got_a, others_a, current, token = lax.optimization_barrier(
            (got_a, others_a, current, token)
        )
        got_b = gather_step(layout, current, GATHER_ORDER, 2)
        others_a += [layout.swap(piece) for piece in got_a[1:]]
        gathered = [(others_a, got_a), None]
        bias_table = None
    else:
        gathered = [([whole], [whole]) for whole in wholes]
        bias_full = lax.all_gather(bias, BOTH, axis=0, tiled=True).astype(F32)
        bias_table = jnp.broadcast_to(bias_full.reshape(width // 128, 1, 128), (width // 128, 8, 128))

    cot_rows = cotangent.reshape(total_nodes, width)
    before = None
    grads, weights = [], []
    results = []
    for j, (start, size) in enumerate(chunks):
        half = size // 2
        last = j == len(chunks) - 1
        if tuned and j == 1:
            reduced, got_b, others_b, before = lax.optimization_barrier(
                ([results[0][1], recv], got_b, others_b, before)
            )
            sums = reduce_step(layout, reduced, back_a, 0)
            reduced_a = reduce_send(layout, reduced, sums, back_a, 0)
            others_b += [layout.swap(piece) for piece in got_b[1:]]
            gathered[1] = (others_b, got_b)
        pair = []
        for side in range(2):
            if tuned and j == 0 and side == 1:
                last_b = jnp.concatenate(got_b)
                last_b, before, pair = lax.optimization_barrier((last_b, before, pair))
                recv = layout.swap(pair[0])
                got_b = gather_step(layout, last_b, GATHER_ORDER, 3)
                others_b = [layout.swap(last_b)]
            if tuned and j == 1 and side == 1:
                reduced_a, before, pair = lax.optimization_barrier((reduced_a, before, pair))
                recv = layout.swap(pair[0])
                sums = reduce_step(layout, reduced_a, back_a, 1)
                reduced_a = reduce_send(layout, reduced_a, sums, back_a, 1)
            took = layer_half(
                start,
                half,
                side,
                tuned and last,
                [tables[0], tables[1], tables[2 + j], tables[4]],
                token,
                mixed,
                mixed_t,
                bias_table,
                cot_rows,
                alive_wide,
                gathered[j][side],
                gathered[j][1] if bias_table is None else [],
                rows,
                before,
                block,
            )
            act, out, bias_sums, grad_part, weight_part = took[:5]
            if len(took) == 6:
                bias_table = took[5]
            before = (bias_sums, act)
            grads.append(grad_part)
            weights.append(weight_part)
            if tuned:
                out = out.reshape(devices // 2, -1, half)
            pair.append(out)
        results.append(pair)

    sizes = [rim] * (shards - 1) + [span] + [rim] * shards
    if tuned:
        reduced_a, reduced_b, before = lax.optimization_barrier(
            (reduced_a, [results[1][1], recv], before)
        )
        sums_a = reduce_step(layout, reduced_a, back_a, 2)
        sums_b = reduce_step(layout, reduced_b, back_b, 0)
        reduced_a = reduce_send(layout, reduced_a, sums_a, back_a, 2)
        reduced_b = reduce_send(layout, reduced_b, sums_b, back_b, 0)
    grad = mixed_grad(scale_wide, grads, weights)
    parts = rim_grads(cnt_t, grad, sizes)
    if tuned:
        reduced_a, reduced_b, parts = lax.optimization_barrier((reduced_a, reduced_b, parts))
        sums_a = reduce_step(layout, reduced_a, back_a, 3)
        sums_b = reduce_step(layout, reduced_b, back_b, 1)
        reduced_a = reduce_send(layout, reduced_a, sums_a, back_a, 3)
        reduced_b = reduce_send(layout, reduced_b, sums_b, back_b, 1)
    cross, far = parts[: shards - 1], parts[shards:]
    near_back = near_swap(parts[shards - 1]).astype(F32)

    def toward(m, k):
        return cross[k - 1][m].astype(F32) + near_back[m, k * rim : (k + 1) * rim]

    hop_0 = [
        from_shard(jnp.concatenate([toward(0, k).astype(BF16), far[k][0]]), k)
        for k in range(1, shards)
    ]
    hop_1 = far_swap(jnp.concatenate([part[1] for part in far]))
    local, head = own_grads(cnt_t, grad, rim)

    if tuned:
        reduced_b, reduced_a, hop_0, hop_1, local, head = lax.optimization_barrier(
            (reduced_b, reduced_a, hop_0, hop_1, local, head)
        )
        sums_b = reduce_step(layout, reduced_b, back_b, 2)
        reduced_b = reduce_send(layout, reduced_b, sums_b, back_b, 2)
        sums_b = reduce_step(layout, reduced_b, back_b, 3)
        reduced_b = reduce_send(layout, reduced_b, sums_b, back_b, 3)
    far_sum = far[0][0].astype(F32) + sum(both[rim:].astype(F32) for both in hop_0)
    back_0 = far_swap(far_sum.astype(BF16)).astype(F32)
    hop_1 = hop_1.astype(F32)
    back_1 = [
        from_shard((toward(1, k) + hop_1[k * rim : (k + 1) * rim]).astype(BF16), k)
        for k in range(1, shards)
    ]
    sum_0 = head[0] + near_back[0, :rim] + sum(both[:rim].astype(F32) for both in hop_0) + back_0
    sum_1 = head[1] + near_back[1, :rim] + hop_1[:rim] + sum(both.astype(F32) for both in back_1)
    head = jnp.stack([sum_0, sum_1]).astype(BF16)
    feature_grad = lax.dynamic_update_slice(local, head, (0, 0, 0))

    weight_grads = []
    for j in range(2):
        if tuned:
            both = sum(part[0].astype(F32) for part in (reduced_a, reduced_b)[j])
            ours, theirs = both[:block], layout.swap(both[block:])
            low_half = jnp.where(core == 0, ours, theirs[:block])
            high_half = jnp.where(core == 0, theirs[:block], ours)
            if j == 1:
                sums = both[2 * block : 2 * block + 8, :128] + theirs[block + 8 :, :128]
                sums = jnp.sum(sums, axis=0)
                bias_out = jnp.where(here["x"] == 0, sums[:own_rows], sums[128 - own_rows :])
        else:
            send, keep = results[j]
            low_half, high_half = (
                lax.psum_scatter(
                    jnp.where(core == which, keep, send), BOTH, scatter_dimension=0, tiled=True
                ).astype(F32)
                for which in (0, 1)
            )
        weight_grads += [low_half, high_half]
    if not tuned:
        bias_sum = jnp.sum(before[0], axis=1).reshape(width)
        bias_out = lax.psum_scatter(bias_sum, BOTH, scatter_dimension=0, tiled=True)

    return (
        before[1].reshape(features.shape),
        feature_grad,
        jnp.concatenate(weight_grads, axis=1),
        bias_out,
    )


def solution(mesh):
    layout = Layout(mesh.shape["blk"], mesh.shape["shard"])
    rows = P(None, BOTH, None)
    return jax.shard_map(
        functools.partial(per_device, layout),
        mesh=mesh,
        in_specs=(rows, P(BOTH, None), P(BOTH), rows, rows, P(None, BOTH)),
        out_specs=(rows, rows, P(BOTH, None), P(BOTH)),
        check_vma=False,
    )
```

```python
import functools

import jax
import jax.numpy as jnp
import numpy as np
from jax import lax
from jax.experimental import pallas as pl
from jax.experimental.pallas import tpu as pltpu
from jax.sharding import PartitionSpec as P

BOTH = ("blk", "shard")
F32 = jnp.float32
BF16 = jnp.bfloat16
MIB = 1 << 20
GELU_A = 0.7978845608028654
GELU_B = 0.044715
HBM = pl.BlockSpec(memory_space=pltpu.HBM)
VMEM = pl.BlockSpec(memory_space=pltpu.VMEM)
SMEM = pl.BlockSpec(memory_space=pltpu.SMEM)

CHUNKS = (0.5, 0.5)
SPLIT_AT = 6
GATHER_ORDER = (("hlxy", "hlyx"),) * 2
REDUCE_ORDER = (("xylh", "yxlh"),) * 2


def cost(us):
    return pl.CostEstimate(flops=int(us * 0.25e9), bytes_accessed=0, transcendentals=0)


def held(array, space):
    return pltpu.with_memory_space_constraint(array, space)


def small_dot(a, b, contract=((1,), (0,))):
    return lax.dot_general(a, b, (contract, ((), ())), preferred_element_type=F32)


def count_kernel(code_ref, cnt_ref, cnt_t_ref):
    node_count, slots = code_ref.shape
    table = cnt_ref.shape[1]
    step = 64
    kind = jnp.int16

    def some_nodes(i, carry):
        at = pl.ds(pl.multiple_of(i * step, step), step)
        codes = code_ref[at, :].astype(kind)
        column = lax.broadcasted_iota(kind, (step, table), 1)
        row = lax.broadcasted_iota(kind, (step, table), 0) + (i * step).astype(kind)
        total = jnp.where(column == row, BF16(2), BF16(0))
        for k in range(slots):
            total = total + jnp.where(column == codes[:, k : k + 1], BF16(1), BF16(0))
        cnt_ref[at, :] = total
        return carry

    lax.fori_loop(0, node_count // step, some_nodes, 0)
    cnt_t_ref[...] = cnt_ref[...].T


def count_tables(codes, table):
    micro, node_count, slots = codes.shape
    return pl.pallas_call(
        count_kernel,
        grid=(micro,),
        in_specs=[pl.BlockSpec((None, node_count, slots), lambda m: (m, 0, 0))],
        out_specs=[
            pl.BlockSpec((None, node_count, table), lambda m: (m, 0, 0)),
            pl.BlockSpec((None, table, node_count), lambda m: (m, 0, 0)),
        ],
        out_shape=[
            jax.ShapeDtypeStruct((micro, node_count, table), BF16),
            jax.ShapeDtypeStruct((micro, table, node_count), BF16),
        ],
        compiler_params=pltpu.CompilerParams(vmem_limit_bytes=24 * MIB),
        cost_estimate=cost(6),
        name="count_tables",
    )(codes)


def mix_kernel(counts, cnt_ref, scale_ref, own_ref, *refs):
    piece_refs, (mixed_ref, mixed_t_ref, token_ref, rim) = refs[:-4], refs[-4:]
    node_count = own_ref.shape[0]
    for micro, count in enumerate(counts):
        first = sum(counts[:micro])

        @pl.when(pl.program_id(0) == micro)
        def _():
            at = 0
            for piece in piece_refs[first : first + count]:
                rim[at : at + piece.shape[0], :] = piece[...]
                at += piece.shape[0]

    total = small_dot(cnt_ref[:, :node_count], own_ref[...])
    total = total + small_dot(cnt_ref[:, node_count:], rim[...])
    scale = jnp.concatenate([scale_ref[...]] * (total.shape[1] // 128), axis=1)
    low = (total * scale).astype(BF16)
    mixed_ref[...] = low
    mixed_t_ref[...] = low.T
    token_ref[...] = jnp.zeros_like(token_ref)


def mix(cnt, scale, features, pieces):
    micro, node_count, width = features.shape
    table = cnt.shape[2]
    wide = min(512, width)

    def rows_of(piece, which):
        return pl.BlockSpec(
            (piece.shape[0], wide), lambda m, j: (0, jnp.where(m == which, j, (micro - 1 - m) * 0))
        )

    return pl.pallas_call(
        functools.partial(mix_kernel, [len(group) for group in pieces]),
        grid=(micro, width // wide),
        in_specs=[
            pl.BlockSpec((None, node_count, table), lambda m, j: (m, 0, 0)),
            pl.BlockSpec((node_count, 128), lambda m, j: (m, 0)),
            pl.BlockSpec((None, node_count, wide), lambda m, j: (m, 0, j)),
        ]
        + [rows_of(piece, which) for which in range(micro) for piece in pieces[which]],
        out_specs=[
            pl.BlockSpec((node_count, wide), lambda m, j: (m, j)),
            pl.BlockSpec((wide, node_count), lambda m, j: (j, m)),
            pl.BlockSpec((8, 128), lambda m, j: (0, 0)),
        ],
        out_shape=[
            pltpu.VMEM((micro * node_count, width), BF16),
            pltpu.VMEM((width, micro * node_count), BF16),
            jax.ShapeDtypeStruct((8, 128), F32),
        ],
        scratch_shapes=[pltpu.VMEM((table - node_count, wide), BF16)],
        compiler_params=pltpu.CompilerParams(vmem_limit_bytes=24 * MIB),
        cost_estimate=cost(6),
        name="mix",
    )(cnt, scale, features, *[piece for group in pieces for piece in group])


def gelu_and_grad(linear, incoming, alive):
    square = linear * linear
    bend = jnp.tanh(linear * (GELU_A + (GELU_A * GELU_B) * square))
    share = 0.5 + 0.5 * bend
    value = linear * share
    slope = share + value * (1.0 - bend) * (GELU_A + (3.0 * GELU_A * GELU_B) * square)
    return (value * alive).astype(BF16), (incoming.astype(F32) * alive * slope).astype(BF16)


def half_kernel(plan, *refs):
    start, half, side, first, tail, keeps, whole, blocks, bias_blocks, inner, rows, tile, sub, block = plan
    refs = list(refs)
    place_ref, chip_ref, slot_ref, half_ref, _, mixed, mixed_t, cot, alive = refs[:9]
    del refs[:9]
    n_pieces = 1 if whole else len(blocks)
    pieces = refs[:n_pieces]
    del refs[:n_pieces]
    bias_pieces = refs[: len(bias_blocks)]
    del refs[: len(bias_blocks)]
    bias = None if bias_blocks else refs.pop(0)
    bias_sums_in = None
    if not first:
        bias_sums_in = refs[0]
        del refs[:2]
    act, out, bias_sums, grad_out, wv = refs[:5]
    del refs[:5]
    bias_out = refs.pop(0) if bias_blocks else None
    cv, av, linear, bias_raw, sem = refs
    node_count, width = mixed.shape
    tiles = half // tile
    mine = half_ref[0]
    holder = mine if side else 1 - mine
    offset = pl.multiple_of(start + holder * half, 128)

    def columns(t):
        return slice(t * tile, (t + 1) * tile)

    def fetch_weights(t):
        if whole:
            part = pl.ds(pl.multiple_of(holder * half + t * tile, 128), tile)
            pltpu.make_async_copy(pieces[0].at[:, part], wv.at[:, columns(t)], sem.at[t]).start()
        at = 0
        for ref, count in zip(pieces, blocks):
            for i in range(count):
                for k in range(inner):
                    into = pl.ds(pl.multiple_of(place_ref[side, at], rows), rows)
                    pltpu.make_async_copy(
                        ref.at[i, k * rows : (k + 1) * rows, columns(t)],
                        wv.at[into, columns(t)],
                        sem.at[t],
                    ).start()
                    at += 1

    fetch_weights(0)
    cot_copy = pltpu.make_async_copy(cot.at[:, pl.ds(offset, half)], cv, sem.at[2 * tiles])
    cot_copy.start()
    for t in range(1, tiles):
        fetch_weights(t)
    seen = 0
    for ref, count in zip(bias_pieces, bias_blocks):
        for i in range(count):
            pltpu.make_async_copy(
                ref.at[i, inner * rows : inner * rows + 16, 0:128],
                bias_raw.at[chip_ref[seen]],
                sem.at[2 * tiles + 1],
            ).start()
            seen += 1

    if first:
        bias_sums[...] = jnp.zeros_like(bias_sums)
    else:
        bias_sums[...] = bias_sums_in[...]
    if bias_blocks:
        pltpu.make_async_copy(bias_raw, bias_raw, sem.at[2 * tiles + 1]).wait()
        for chip in range(bias_raw.shape[0] // 2):
            pair = bias_raw[2 * chip].astype(F32) + bias_raw[2 * chip + 1].astype(F32)
            bias_out[2 * chip] = jnp.where(mine == 0, pair[:8], pair[8:])
            bias_out[2 * chip + 1] = jnp.where(mine == 0, pair[8:], pair[:8])
        bias = bias_out

    blocks_of_rows = range(0, node_count, sub)

    def run_linear(t, m):
        linear[t % 2, m : m + sub, :] = small_dot(mixed[m : m + sub, :], wv[:, columns(t)])

    def run_gelu(t):
        group = offset // 128 + t * (tile // 128)
        shift = jnp.concatenate([bias[group + k] for k in range(tile // 128)], axis=1)[:1]
        total = jnp.zeros((8, tile), F32)
        step = 64
        for m in range(0, node_count, step):
            live = jnp.concatenate([alive[m : m + step, :]] * (tile // 128), axis=1)
            value, grad = gelu_and_grad(
                linear[t % 2, m : m + step, :] + shift, cv[m : m + step, columns(t)], live
            )
            av[m : m + step, columns(t)] = value
            grad_out[m : m + step, columns(t)] = grad
            total = total + jnp.sum(grad.astype(F32).reshape(step // 8, 8, tile), axis=0)
        for k in range(tile // 128):
            bias_sums[group + k] = total[:, k * 128 : (k + 1) * 128]

    def run_weight_grad(t):
        for m in range(0, width, sub):
            part = small_dot(mixed_t[m : m + sub, :], grad_out[:, columns(t)]).astype(BF16)
            for b in range(0, sub, block):
                into = pl.multiple_of(slot_ref[side, (m + b) // block], 16)
                out[pl.ds(into, block), columns(t)] = part[b : b + block]

    outs = []

    def write_out(t):
        part = pl.ds(pl.multiple_of(offset + t * tile, 128), tile)
        copy = pltpu.make_async_copy(av.at[:, columns(t)], act.at[:, part], sem.at[tiles + t])
        copy.start()
        outs.append(copy)

    def write_tail():
        for pair in range(width // block // 2):
            chip = pair // 2
            base = slot_ref[side, chip * 4 + pair % 2] - holder * block
            if keeps:
                both = jnp.concatenate(
                    [bias_sums[2 * chip + holder], bias_sums[2 * chip + 1 - holder]], axis=0
                )
                both = jnp.concatenate([both, jnp.zeros((16, half - 128), F32)], axis=1)
            else:
                both = jnp.zeros((16, half), F32)
            out[pl.ds(pl.multiple_of(base + 2 * block, 16), 16), :] = both.astype(BF16)

    def wait_weights(t):
        pltpu.make_async_copy(wv.at[:, columns(t)], wv.at[:, columns(t)], sem.at[t]).wait()

    wait_weights(0)
    for m in blocks_of_rows:
        run_linear(0, m)
    cot_copy.wait()
    for t in range(tiles):
        if t + 1 < tiles:
            wait_weights(t + 1)
            for m in blocks_of_rows:
                run_linear(t + 1, m)
        run_gelu(t)
        if t + 1 == tiles and tail:
            write_tail()
        write_out(t)
        run_weight_grad(t)
    for copy in outs:
        copy.wait()


def layer_half(
    start, half, side, tail, tables, token, mixed, mixed_t, bias, cot, alive, pieces, bias_pieces, rows, before, block
):
    node_count, width = mixed.shape
    first = before is None
    tile = min(256, half)
    sub = min(512, node_count)
    groups = width // 128
    out_rows = width + 16 * (width // block // 2) if tail else width
    plan = (
        start,
        half,
        side,
        first,
        tail,
        tail and side == 1,
        pieces[0].ndim == 2,
        [piece.shape[0] for piece in pieces if piece.ndim == 3],
        [piece.shape[0] for piece in bias_pieces],
        2,
        rows,
        tile,
        sub,
        block,
    )
    operands = [*tables, token]
    operands += [held(array, pltpu.VMEM) for array in (mixed, mixed_t)]
    operands += [held(cot, pltpu.HBM), alive]
    operands += [held(array, pltpu.HBM) for array in (*pieces, *bias_pieces)]
    specs = [SMEM] * 4 + [HBM, VMEM, VMEM, HBM, VMEM] + [HBM] * (len(pieces) + len(bias_pieces))
    if not bias_pieces:
        operands.append(bias)
        specs.append(VMEM)
    aliases = {}
    if not first:
        operands += list(before)
        specs += [VMEM, HBM]
        aliases = {len(operands) - 1: 0}
    out_specs = [HBM, VMEM, VMEM, VMEM, VMEM]
    out_shape = [
        pltpu.HBM((node_count, width), BF16),
        pltpu.VMEM((out_rows, half), BF16),
        jax.ShapeDtypeStruct((groups, 8, 128), F32),
        pltpu.VMEM((node_count, half), BF16),
        pltpu.VMEM((width, half), BF16),
    ]
    if bias_pieces:
        out_specs.append(VMEM)
        out_shape.append(jax.ShapeDtypeStruct((groups, 8, 128), F32))
    return pl.pallas_call(
        functools.partial(half_kernel, plan),
        in_specs=specs,
        out_specs=out_specs,
        out_shape=out_shape,
        scratch_shapes=[
            pltpu.VMEM((node_count, half), BF16),
            pltpu.VMEM((node_count, half), BF16),
            pltpu.VMEM((2, node_count, tile), F32),
            pltpu.VMEM((groups, 16, 128), BF16),
            pltpu.SemaphoreType.DMA((2 * (half // tile) + 2,)),
        ],
        input_output_aliases=aliases,
        compiler_params=pltpu.CompilerParams(vmem_limit_bytes=16 * MIB),
        cost_estimate=cost(8),
        name="layer_half",
    )(*operands)


def mixed_grad_kernel(count, scale, *refs):
    grads, weights, (out, token) = refs[:count], refs[count : 2 * count], refs[2 * count :]
    token[...] = jnp.zeros_like(token)
    node_count, width = out.shape
    tile = min(256, width)
    sub = min(512, node_count)
    for d in range(0, width, tile):
        for m in range(0, node_count, sub):
            part = sum(
                small_dot(grad[m : m + sub, :], weight[d : d + tile, :], ((1,), (1,)))
                for grad, weight in zip(grads, weights)
            )
            part = part * jnp.concatenate([scale[m : m + sub, :]] * (tile // 128), axis=1)
            out[m : m + sub, d : d + tile] = part.astype(BF16)


def mixed_grad(scale, grads, weights):
    node_count, width = grads[0].shape[0], weights[0].shape[0]
    return pl.pallas_call(
        functools.partial(mixed_grad_kernel, len(grads)),
        in_specs=[VMEM] * (1 + 2 * len(grads)),
        out_specs=[VMEM, VMEM],
        out_shape=[
            jax.ShapeDtypeStruct((node_count, width), BF16),
            jax.ShapeDtypeStruct((8, 128), F32),
        ],
        compiler_params=pltpu.CompilerParams(vmem_limit_bytes=16 * MIB),
        cost_estimate=cost(10),
        name="mixed_grad",
    )(scale, *[held(array, pltpu.VMEM) for array in (*grads, *weights)])


def rim_grad_kernel(sizes, cnt_t_ref, grad_ref, *outs):
    node_count = grad_ref.shape[0]
    part = small_dot(cnt_t_ref[node_count:, :], grad_ref[...])
    at = 0
    for out, rows in zip(outs, sizes):
        out[...] = part[at : at + rows].astype(BF16)
        at += rows


def rim_grads(cnt_t, grad, sizes):
    micro, table, node_count = cnt_t.shape
    width = grad.shape[1]
    wide = min(512, width)
    return pl.pallas_call(
        functools.partial(rim_grad_kernel, sizes),
        grid=(micro, width // wide),
        in_specs=[
            pl.BlockSpec((None, table, node_count), lambda m, j: (m, 0, 0)),
            pl.BlockSpec((node_count, wide), lambda m, j: (m, j)),
        ],
        out_specs=[pl.BlockSpec((None, rows, wide), lambda m, j: (m, 0, j)) for rows in sizes],
        out_shape=[jax.ShapeDtypeStruct((micro, rows, width), BF16) for rows in sizes],
        compiler_params=pltpu.CompilerParams(vmem_limit_bytes=24 * MIB),
        cost_estimate=cost(3),
        name="rim_grads",
    )(cnt_t, grad)


def own_grad_kernel(cnt_t_ref, grad_ref, out_ref, head_ref):
    part = small_dot(cnt_t_ref[...], grad_ref[...])
    out_ref[...] = part.astype(BF16)
    head_ref[...] = part[: head_ref.shape[0]]


def own_grads(cnt_t, grad, rim_size):
    micro, _, node_count = cnt_t.shape
    width = grad.shape[1]
    wide = min(512, width)
    return pl.pallas_call(
        own_grad_kernel,
        grid=(micro, width // wide),
        in_specs=[
            pl.BlockSpec((None, node_count, node_count), lambda m, j: (m, 0, 0)),
            pl.BlockSpec((node_count, wide), lambda m, j: (m, j)),
        ],
        out_specs=[
            pl.BlockSpec((None, node_count, wide), lambda m, j: (m, 0, j)),
            pl.BlockSpec((None, rim_size, wide), lambda m, j: (m, 0, j)),
        ],
        out_shape=[
            jax.ShapeDtypeStruct((micro, node_count, width), BF16),
            jax.ShapeDtypeStruct((micro, rim_size, width), F32),
        ],
        compiler_params=pltpu.CompilerParams(vmem_limit_bytes=24 * MIB),
        cost_estimate=cost(4),
        name="own_grads",
    )(cnt_t, grad)


class Layout:
    def __init__(self, blks, shards):
        self.blks, self.shards = blks, shards
        self.tuned = shards == 2 and blks == 16
        self.sizes = {"h": blks // 8, "l": 2, "y": 2, "c": 2, "x": shards}

    def number(self, at):
        blk = ((at["h"] * 2 + at["l"]) * 2 + at["y"]) * 2 + at["c"]
        return blk * self.shards + at["x"]

    def place(self, blk, shard):
        return {"h": blk // 8, "l": blk // 4 % 2, "y": blk // 2 % 2, "c": blk % 2, "x": shard}

    def here(self):
        return self.place(lax.axis_index("blk"), lax.axis_index("shard"))

    def spots(self):
        for number in range(self.blks * self.shards):
            yield self.place(number // self.shards, number % self.shards)

    def flip(self, value, axes):
        pairs = []
        for spot in self.spots():
            there = {axis: at ^ (axis in axes[spot["c"]]) for axis, at in spot.items()}
            pairs.append((self.number(spot), self.number(there)))
        return lax.ppermute(value, BOTH, pairs)

    def swap(self, value):
        return self.flip(value, "cc")


def from_shard(value, by):
    count = lax.axis_size("shard")
    return lax.ppermute(value, "shard", [(i, (i + by) % count) for i in range(count)])


def near_swap(value):
    count = lax.axis_size("blk")
    return lax.ppermute(value, "blk", [(i, i ^ 1) for i in range(count)])


def far_swap(value):
    count = lax.axis_size("blk")
    return lax.ppermute(value, "blk", [(i, (i + (1 if i % 2 else -1)) % count) for i in range(count)])


def tie(value, *others):
    return lax.optimization_barrier((value, others))[0]


def gather_step(layout, current, orders, step):
    return [current, layout.flip(current, (orders[0][step], orders[1][step]))]


def reduce_step(layout, parts, orders, step):
    size = parts[0].shape[0] // 2
    total = sum(part[:size].astype(F32) for part in parts).astype(BF16)
    got = layout.flip(total, (orders[0][step], orders[1][step]))
    return [part[size:] for part in parts] + [got]


def gathered_from(layout, order, bases):
    current = [{"c": b} for b in range(bases)]
    for axis in order:
        current = [dict(entry, **{axis: k}) for k in range(layout.sizes[axis]) for entry in current]
    return current


def gathered_numbers(layout, orders, bases, here, swapped):
    core = here["c"] ^ 1 if swapped else here["c"]
    tables = []
    for order in orders:
        entries = gathered_from(layout, order, bases)
        tables.append({axis: np.array([e[axis] for e in entries], np.int32) for axis in "hlycx"})
    back = {axis: jnp.where(core == 0, tables[0][axis], tables[1][axis]) for axis in "hlycx"}
    at = {axis: (here[axis] - back[axis]) % layout.sizes[axis] for axis in "hlyx"}
    at["c"] = core ^ back["c"]
    return layout.number(at)


def slots_of(layout, orders, here, swapped):
    core = here["c"] ^ 1 if swapped else here["c"]
    number = np.arange(layout.blks * layout.shards)
    at = layout.place(number // layout.shards, number % layout.shards)
    results = []
    for order in orders:
        slot = 0
        for axis in order:
            count = layout.sizes[axis]
            ahead = (at[axis] - here[axis]) % count
            slot = slot * count + (ahead - 1) % count
        results.append(slot * 2 + (at["c"] ^ core))
    return jnp.where(core == 0, results[0], results[1]).astype(jnp.int32)


class Flow:
    def __init__(self, tied):
        self.tied, self.values, self.fresh = tied, {}, set()

    def __getitem__(self, name):
        return self.values[name]

    def __setitem__(self, name, value):
        self.values[name] = value
        self.fresh.add(name)

    def seal(self, *names):
        names = names or sorted(self.fresh, key=str)
        if self.tied and names:
            made = lax.optimization_barrier([self.values[name] for name in names])
            self.values.update(zip(names, made))
        self.fresh -= set(names)


def per_device(layout, features, weight, bias, cotangent, neighbours, live_count):
    micro_count, node_count, width = features.shape
    shards = layout.shards
    devices = layout.blks * shards
    rim = node_count // 8
    span = shards * rim
    own_rows = weight.shape[0]
    here = layout.here()
    core = here["c"]
    tuned = layout.tuned and own_rows * shards == 128
    chunks = []
    at = 0
    for share in CHUNKS:
        chunks.append((at, int(width * share)))
        at += int(width * share)
    flow = Flow(tuned)

    def gather(j, step):
        if not tuned:
            return
        order = GATHER_ORDER[j]

        def flip(blocks, at):
            return layout.flip(blocks, (order[0][at], order[1][at]))

        if step < 2:
            flow["blocks", j] = jnp.concatenate(
                [flow["blocks", j], flip(flow["blocks", j], step)]
            )
        elif step == 2:
            flow["third", j] = flip(flow["blocks", j], 2)
            flow["fourth", j] = flip(flow["blocks", j], 3)
        else:
            flow["last", j] = flip(flow["third", j], 3)

    NAMES = ("blocks", "third", "fourth", "last")

    def swap_pieces(j, *which):
        if tuned:
            for k in which:
                flow["others", j, k] = layout.swap(flow[NAMES[k], j])

    def swap_out(j):
        if tuned:
            flow["parts", j] = [layout.swap(flow["out", j, 0])]

    def reduce(j, step):
        if tuned:
            flow["parts", j] = reduce_step(layout, flow["parts", j], REDUCE_ORDER[j], step)

    def add_and_flip(parts, order, step):
        total = sum(part.astype(F32) for part in parts).astype(BF16)
        return layout.flip(total, (order[0][step], order[1][step]))

    def reduce_first(j, begin, end):
        if tuned:
            parts = [flow["out", j, 1], *flow["parts", j]]
            flow["first", j, begin] = add_and_flip(
                [part[begin:end] for part in parts], REDUCE_ORDER[j], 0
            )

    def reduce_second(j, split):
        if tuned:
            parts = [flow["out", j, 1], *flow["parts", j]]
            size = parts[0].shape[0] // 4
            early = flow["first", j, 0]
            late = add_and_flip([part[split : 2 * size] for part in parts], REDUCE_ORDER[j], 0)
            got = add_and_flip(
                [part[2 * size : 3 * size] for part in parts] + [early[:size]], REDUCE_ORDER[j], 1
            )
            flow["parts", j] = [part[3 * size :] for part in parts] + [got]
            flow["split", j] = [early[size:], late]

    def reduce_third(j):
        if tuned:
            early, late = flow["split", j]
            parts = flow["parts", j]
            size = parts[0].shape[0] // 2
            got = add_and_flip([part[:size] for part in parts] + [early], REDUCE_ORDER[j], 2)
            flow["parts", j] = [part[size:] for part in parts] + [late, got]

    rim_own = features[:, :rim]
    flow["far"] = far_swap(rim_own)
    flow["cross"] = [from_shard(rim_own, shards - k) for k in range(1, shards)]

    if tuned:
        block = rows = own_rows
        numbers = [
            [gathered_numbers(layout, order, 2, here, flag) for flag in (True, False)]
            for order in GATHER_ORDER
        ]
        places = [jnp.stack(pair) * own_rows for pair in numbers]
        numbers = numbers[0][1]
        chip = (numbers // 4 * 2 + numbers % 2)[::2]
        slots = [
            jnp.stack([slots_of(layout, order, here, flag) for flag in (True, False)])
            for order in REDUCE_ORDER
        ]
        slots = [
            slot // 2 * (2 * block + (16 if j + 1 == len(chunks) else 0)) + slot % 2 * block
            for j, slot in enumerate(slots)
        ]
        halves = [
            jnp.concatenate([weight[:, s + h * n // 2 : s + (h + 1) * n // 2] for s, n in chunks], axis=1)
            for h in range(2)
        ]
        lane = jnp.where(
            here["x"] == 0, jnp.pad(bias, (0, 128 - own_rows)), jnp.pad(bias, (128 - own_rows, 0))
        )
        bias_block = jnp.broadcast_to(jnp.pad(lane, (0, width // 2 - 128))[None], (8, width // 2))
        ours = jnp.where(core == 0, halves[0], halves[1])
        theirs = layout.swap(
            jnp.concatenate([jnp.where(core == 0, halves[1], halves[0]), bias_block], axis=0)
        )
        at = 0
        for j, (_, size) in enumerate(chunks):
            cols = slice(at, at + size // 2)
            blocks = [ours[:, cols], theirs[:own_rows, cols]]
            if j == 0:
                blocks += [bias_block[:, cols], theirs[own_rows:, cols]]
            flow["blocks", j] = jnp.concatenate(blocks, axis=0)[None]
            at += size // 2
        flow["bias"] = None
    else:
        block = rows = 64
        places = [jnp.zeros((2, 1), jnp.int32)] * len(chunks)
        chip = jnp.zeros((2,), jnp.int32)
        slots = [
            jnp.broadcast_to(jnp.arange(0, width, block, dtype=jnp.int32), (2, width // block))
        ] * len(chunks)
        theirs = weight
        for j, (start, size) in enumerate(chunks):
            whole = lax.all_gather(weight[:, start : start + size], BOTH, axis=0, tiled=True)
            flow["pieces", j] = [whole]
        bias_full = lax.all_gather(bias, BOTH, axis=0, tiled=True).astype(F32)
        flow["bias"] = jnp.broadcast_to(
            bias_full.reshape(width // 128, 1, 128), (width // 128, 8, 128)
        )
    tables = (places, chip, slots, core.reshape(1))
    tables = jax.tree.map(lambda array: array.astype(jnp.int32), tables)
    neighbours, tables = tie((neighbours, tables), theirs)
    places, chip, slots, core_table = tables

    gather(0, 0)

    table = node_count + (3 * shards - 1) * rim
    shifted = neighbours - node_count
    section = shifted // span
    ahead = (shifted // rim % shards - here["x"]) % shards
    near_section = jnp.where(core == 0, 2, 1)
    base_slot = jnp.where(
        section == 0,
        node_count - rim,
        jnp.where(section == near_section, node_count + span - rim, node_count + 2 * span - rim),
    )
    slot = base_slot + ahead * rim + shifted % rim
    slot = jnp.where((section == 0) & (ahead == 0), shifted % rim, slot)
    codes = jnp.where(neighbours < node_count, neighbours, slot)
    degree = jnp.sum((neighbours >= 0).astype(F32), axis=2)
    alive = (jnp.arange(node_count, dtype=jnp.int32)[None, :] < live_count).astype(F32)
    weighting = alive / (degree + 1.0)
    total_nodes = micro_count * node_count
    flow["alive"] = jnp.broadcast_to(alive.reshape(total_nodes, 1), (total_nodes, 128))
    flow["scale"] = jnp.broadcast_to(weighting.reshape(total_nodes, 1), (total_nodes, 128))
    flow["cnt"], flow["cnt_t"] = count_tables(codes, table)
    flow.seal()

    gather(0, 1)
    far, cross = flow["far"], flow["cross"]
    flow["far_cross_0"] = [from_shard(far[0], shards - k) for k in range(1, shards)]
    flow["far_cross_1"] = far_swap(jnp.concatenate([rows_of[1] for rows_of in cross]))
    flow["near"] = near_swap(jnp.concatenate([rim_own, *cross], axis=1))
    if tuned:
        flow["blocks", 1] = flow["blocks", 1]
    flow.seal()

    gather(0, 2)
    gather(1, 0)
    mixed, mixed_t, flow["token"] = mix(
        flow["cnt"],
        flow["scale"],
        features,
        [
            [*(rows_of[m] for rows_of in cross), flow["near"][m], far[m], *others]
            for m, others in enumerate((flow["far_cross_0"], [flow["far_cross_1"]]))
        ],
    )
    flow.seal()

    gather(0, 3)
    swap_pieces(0, 0, 1, 2)
    gather(1, 1)
    flow.seal()

    cot_rows = cotangent.reshape(total_nodes, width)
    grads, weights = [], []
    flow["before"] = None

    def half_layer(j, side):
        start, size = chunks[j]
        half = size // 2
        if tuned:
            mine = [flow[name, j] for name in NAMES]
            pieces = mine if side else [flow["others", j, k] for k in range(len(mine))]
            bias_pieces = mine if flow["bias"] is None else []
        else:
            pieces, bias_pieces = flow["pieces", j], []
        took = layer_half(
            start,
            half,
            side,
            tuned and j + 1 == len(chunks),
            [places[j], chip, slots[j], core_table],
            flow["token"],
            mixed,
            mixed_t,
            flow["bias"],
            cot_rows,
            flow["alive"],
            pieces,
            bias_pieces,
            rows,
            flow["before"],
            block,
        )
        act, out, bias_sums, grad_part, weight_part = took[:5]
        if len(took) == 6:
            flow["bias"] = took[5]
        flow["before"] = (bias_sums, act)
        grads.append(grad_part)
        weights.append(weight_part)
        flow["out", j, side] = out.reshape(devices // 2, -1, half) if tuned else out

    gather(1, 2)
    swap_pieces(0, 3)
    half_layer(0, 0)
    flow.seal()

    gather(1, 3)
    swap_pieces(1, 0, 1, 2)
    swap_out(0)
    half_layer(0, 1)
    flow.seal()

    reduce_first(0, 0, SPLIT_AT)
    swap_pieces(1, 3)
    half_layer(1, 0)
    flow.seal()

    reduce_second(0, SPLIT_AT)
    swap_out(1)
    half_layer(1, 1)
    flow.seal()

    reduce_first(1, 0, SPLIT_AT)
    reduce_third(0)
    sizes = [rim] * (shards - 1) + [span] + [rim] * shards
    grad, flow["after_grad"] = mixed_grad(flow["scale"], grads, weights)
    flow["before_grad"] = flow["cnt_t"]
    flow.seal()

    reduce_second(1, SPLIT_AT)
    reduce(0, 3)
    flow["rims"] = rim_grads(flow["before_grad"], grad, sizes)
    parts = flow["rims"]
    cross, far = parts[: shards - 1], parts[shards:]
    near_back = near_swap(parts[shards - 1]).astype(F32)

    def toward(m, k):
        return cross[k - 1][m].astype(F32) + near_back[m, k * rim : (k + 1) * rim]

    flow["hop_0"] = [
        from_shard(jnp.concatenate([toward(0, k).astype(BF16), far[k][0]]), k)
        for k in range(1, shards)
    ]
    flow["hop_1"] = far_swap(jnp.concatenate([part[1] for part in far]))
    if tuned:
        flow["cnt_t"] = flow["cnt_t"]
        flow.seal(("parts", 1), ("split", 1), "cnt_t")
    reduce_third(1)
    flow["local"], flow["head"] = own_grads(flow["cnt_t"], grad, rim)
    flow.seal()

    hop_0, hop_1, head = flow["hop_0"], flow["hop_1"].astype(F32), flow["head"]
    far_sum = far[0][0].astype(F32) + sum(both[rim:].astype(F32) for both in hop_0)
    back_0 = far_swap(far_sum.astype(BF16)).astype(F32)
    back_1 = [
        from_shard((toward(1, k) + hop_1[k * rim : (k + 1) * rim]).astype(BF16), k)
        for k in range(1, shards)
    ]
    reduce(1, 3)
    sum_0 = head[0] + near_back[0, :rim] + sum(both[:rim].astype(F32) for both in hop_0) + back_0
    sum_1 = head[1] + near_back[1, :rim] + hop_1[:rim] + sum(both.astype(F32) for both in back_1)
    head = jnp.stack([sum_0, sum_1]).astype(BF16)
    feature_grad = lax.dynamic_update_slice(flow["local"], head, (0, 0, 0))

    weight_grads = []
    for j in range(len(chunks)):
        if tuned:
            both = sum(part[0].astype(F32) for part in flow["parts", j])
            ours, theirs = both[:block], layout.swap(both[block:])
            low_half = jnp.where(core == 0, ours, theirs[:block])
            high_half = jnp.where(core == 0, theirs[:block], ours)
            if j + 1 == len(chunks):
                sums = both[2 * block : 2 * block + 8, :128] + theirs[block + 8 :, :128]
                sums = jnp.sum(sums, axis=0)
                bias_out = jnp.where(here["x"] == 0, sums[:own_rows], sums[128 - own_rows :])
        else:
            send, keep = flow["out", j, 0], flow["out", j, 1]
            low_half, high_half = (
                lax.psum_scatter(
                    jnp.where(core == which, keep, send), BOTH, scatter_dimension=0, tiled=True
                ).astype(F32)
                for which in (0, 1)
            )
        weight_grads += [low_half, high_half]
    bias_sums, act = flow["before"]
    if not tuned:
        bias_sum = jnp.sum(bias_sums, axis=1).reshape(width)
        bias_out = lax.psum_scatter(bias_sum, BOTH, scatter_dimension=0, tiled=True)

    return (
        act.reshape(features.shape),
        feature_grad,
        jnp.concatenate(weight_grads, axis=1),
        bias_out,
    )


def solution(mesh):
    layout = Layout(mesh.shape["blk"], mesh.shape["shard"])
    rows = P(None, BOTH, None)
    return jax.shard_map(
        functools.partial(per_device, layout),
        mesh=mesh,
        in_specs=(rows, P(BOTH, None), P(BOTH), rows, rows, P(None, BOTH)),
        out_specs=(rows, rows, P(BOTH, None), P(BOTH)),
        check_vma=False,
    )
```

```python
import functools

import jax
import jax.numpy as jnp
import numpy as np
from jax import lax
from jax.experimental import pallas as pl
from jax.experimental.pallas import tpu as pltpu
from jax.sharding import PartitionSpec as P

BOTH = ("blk", "shard")
F32 = jnp.float32
BF16 = jnp.bfloat16
MIB = 1 << 20
GELU_A = 0.7978845608028654
GELU_B = 0.044715
HBM = pl.BlockSpec(memory_space=pltpu.HBM)
VMEM = pl.BlockSpec(memory_space=pltpu.VMEM)
SMEM = pl.BlockSpec(memory_space=pltpu.SMEM)

CHUNKS = (0.5, 0.5)
SPLIT_AT = (6, 8)
GATHER_ORDER = (("hlxy", "hlyx"),) * 2
REDUCE_ORDER = (("xylh", "yxlh"),) * 2


def cost(us):
    return pl.CostEstimate(flops=int(us * 0.25e9), bytes_accessed=0, transcendentals=0)


def held(array, space):
    return pltpu.with_memory_space_constraint(array, space)


def small_dot(a, b, contract=((1,), (0,))):
    return lax.dot_general(a, b, (contract, ((), ())), preferred_element_type=F32)


def count_kernel(code_ref, cnt_ref, cnt_t_ref):
    node_count, slots = code_ref.shape
    table = cnt_ref.shape[1]
    step = 64
    kind = jnp.int16

    def some_nodes(i, carry):
        at = pl.ds(pl.multiple_of(i * step, step), step)
        codes = code_ref[at, :].astype(kind)
        column = lax.broadcasted_iota(kind, (step, table), 1)
        row = lax.broadcasted_iota(kind, (step, table), 0) + (i * step).astype(kind)
        total = jnp.where(column == row, BF16(2), BF16(0))
        for k in range(slots):
            total = total + jnp.where(column == codes[:, k : k + 1], BF16(1), BF16(0))
        cnt_ref[at, :] = total
        return carry

    lax.fori_loop(0, node_count // step, some_nodes, 0)
    cnt_t_ref[...] = cnt_ref[...].T


def count_tables(codes, table):
    micro, node_count, slots = codes.shape
    return pl.pallas_call(
        count_kernel,
        grid=(micro,),
        in_specs=[pl.BlockSpec((None, node_count, slots), lambda m: (m, 0, 0))],
        out_specs=[
            pl.BlockSpec((None, node_count, table), lambda m: (m, 0, 0)),
            pl.BlockSpec((None, table, node_count), lambda m: (m, 0, 0)),
        ],
        out_shape=[
            jax.ShapeDtypeStruct((micro, node_count, table), BF16),
            jax.ShapeDtypeStruct((micro, table, node_count), BF16),
        ],
        compiler_params=pltpu.CompilerParams(vmem_limit_bytes=24 * MIB),
        cost_estimate=cost(6),
        name="count_tables",
    )(codes)


def mix_kernel(counts, cnt_ref, scale_ref, own_ref, *refs):
    piece_refs, (mixed_ref, mixed_t_ref, token_ref, rim) = refs[:-4], refs[-4:]
    node_count = own_ref.shape[0]
    for micro, count in enumerate(counts):
        first = sum(counts[:micro])

        @pl.when(pl.program_id(0) == micro)
        def _():
            at = 0
            for piece in piece_refs[first : first + count]:
                rim[at : at + piece.shape[0], :] = piece[...]
                at += piece.shape[0]

    total = small_dot(cnt_ref[:, :node_count], own_ref[...])
    total = total + small_dot(cnt_ref[:, node_count:], rim[...])
    scale = jnp.concatenate([scale_ref[...]] * (total.shape[1] // 128), axis=1)
    low = (total * scale).astype(BF16)
    mixed_ref[...] = low
    mixed_t_ref[...] = low.T
    token_ref[...] = jnp.zeros_like(token_ref)


def mix(cnt, scale, features, pieces):
    micro, node_count, width = features.shape
    table = cnt.shape[2]
    wide = min(512, width)

    def rows_of(piece, which):
        return pl.BlockSpec(
            (piece.shape[0], wide), lambda m, j: (0, jnp.where(m == which, j, (micro - 1 - m) * 0))
        )

    return pl.pallas_call(
        functools.partial(mix_kernel, [len(group) for group in pieces]),
        grid=(micro, width // wide),
        in_specs=[
            pl.BlockSpec((None, node_count, table), lambda m, j: (m, 0, 0)),
            pl.BlockSpec((node_count, 128), lambda m, j: (m, 0)),
            pl.BlockSpec((None, node_count, wide), lambda m, j: (m, 0, j)),
        ]
        + [rows_of(piece, which) for which in range(micro) for piece in pieces[which]],
        out_specs=[
            pl.BlockSpec((node_count, wide), lambda m, j: (m, j)),
            pl.BlockSpec((wide, node_count), lambda m, j: (j, m)),
            pl.BlockSpec((8, 128), lambda m, j: (0, 0)),
        ],
        out_shape=[
            pltpu.VMEM((micro * node_count, width), BF16),
            pltpu.VMEM((width, micro * node_count), BF16),
            jax.ShapeDtypeStruct((8, 128), F32),
        ],
        scratch_shapes=[pltpu.VMEM((table - node_count, wide), BF16)],
        compiler_params=pltpu.CompilerParams(vmem_limit_bytes=24 * MIB),
        cost_estimate=cost(6),
        name="mix",
    )(cnt, scale, features, *[piece for group in pieces for piece in group])


def gelu_and_grad(linear, incoming, alive):
    square = linear * linear
    bend = jnp.tanh(linear * (GELU_A + (GELU_A * GELU_B) * square))
    share = 0.5 + 0.5 * bend
    value = linear * share
    slope = share + value * (1.0 - bend) * (GELU_A + (3.0 * GELU_A * GELU_B) * square)
    return (value * alive).astype(BF16), (incoming.astype(F32) * alive * slope).astype(BF16)


def half_kernel(plan, *refs):
    start, half, side, first, tail, keeps, whole, blocks, bias_blocks, inner, rows, tile, sub, block = plan
    refs = list(refs)
    place_ref, chip_ref, slot_ref, half_ref, _, mixed, mixed_t, cot, alive = refs[:9]
    del refs[:9]
    n_pieces = 1 if whole else len(blocks)
    pieces = refs[:n_pieces]
    del refs[:n_pieces]
    bias_pieces = refs[: len(bias_blocks)]
    del refs[: len(bias_blocks)]
    bias = None if bias_blocks else refs.pop(0)
    bias_sums_in = None
    if not first:
        bias_sums_in = refs[0]
        del refs[:2]
    act, out, bias_sums, grad_out, wv = refs[:5]
    del refs[:5]
    bias_out = refs.pop(0) if bias_blocks else None
    cv, av, linear, bias_raw, sem = refs
    node_count, width = mixed.shape
    tiles = half // tile
    mine = half_ref[0]
    holder = mine if side else 1 - mine
    offset = pl.multiple_of(start + holder * half, 128)

    def columns(t):
        return slice(t * tile, (t + 1) * tile)

    def fetch_weights(t):
        if whole:
            part = pl.ds(pl.multiple_of(holder * half + t * tile, 128), tile)
            pltpu.make_async_copy(pieces[0].at[:, part], wv.at[:, columns(t)], sem.at[t]).start()
        at = 0
        for ref, count in zip(pieces, blocks):
            for i in range(count):
                for k in range(inner):
                    into = pl.ds(pl.multiple_of(place_ref[side, at], rows), rows)
                    pltpu.make_async_copy(
                        ref.at[i, k * rows : (k + 1) * rows, columns(t)],
                        wv.at[into, columns(t)],
                        sem.at[t],
                    ).start()
                    at += 1

    fetch_weights(0)
    cot_copy = pltpu.make_async_copy(cot.at[:, pl.ds(offset, half)], cv, sem.at[2 * tiles])
    cot_copy.start()
    for t in range(1, tiles):
        fetch_weights(t)
    seen = 0
    for ref, count in zip(bias_pieces, bias_blocks):
        for i in range(count):
            for k in range(inner // 2):
                pltpu.make_async_copy(
                    ref.at[i, inner * rows : inner * rows + 16, k * 128 : (k + 1) * 128],
                    bias_raw.at[chip_ref[seen]],
                    sem.at[2 * tiles + 1],
                ).start()
                seen += 1

    if first:
        bias_sums[...] = jnp.zeros_like(bias_sums)
    else:
        bias_sums[...] = bias_sums_in[...]
    if bias_blocks:
        pltpu.make_async_copy(bias_raw, bias_raw, sem.at[2 * tiles + 1]).wait()
        for chip in range(bias_raw.shape[0] // 2):
            pair = bias_raw[2 * chip].astype(F32) + bias_raw[2 * chip + 1].astype(F32)
            bias_out[2 * chip] = jnp.where(mine == 0, pair[:8], pair[8:])
            bias_out[2 * chip + 1] = jnp.where(mine == 0, pair[8:], pair[:8])
        bias = bias_out

    blocks_of_rows = range(0, node_count, sub)

    def run_linear(t, m):
        linear[t % 2, m : m + sub, :] = small_dot(mixed[m : m + sub, :], wv[:, columns(t)])

    def run_gelu(t):
        group = offset // 128 + t * (tile // 128)
        shift = jnp.concatenate([bias[group + k] for k in range(tile // 128)], axis=1)[:1]
        total = jnp.zeros((8, tile), F32)
        step = 64
        for m in range(0, node_count, step):
            live = jnp.concatenate([alive[m : m + step, :]] * (tile // 128), axis=1)
            value, grad = gelu_and_grad(
                linear[t % 2, m : m + step, :] + shift, cv[m : m + step, columns(t)], live
            )
            av[m : m + step, columns(t)] = value
            grad_out[m : m + step, columns(t)] = grad
            total = total + jnp.sum(grad.astype(F32).reshape(step // 8, 8, tile), axis=0)
        for k in range(tile // 128):
            bias_sums[group + k] = total[:, k * 128 : (k + 1) * 128]

    def run_weight_grad(t):
        for m in range(0, width, sub):
            part = small_dot(mixed_t[m : m + sub, :], grad_out[:, columns(t)]).astype(BF16)
            for b in range(0, sub, block):
                into = pl.multiple_of(slot_ref[side, (m + b) // block], 16)
                out[pl.ds(into, block), columns(t)] = part[b : b + block]

    outs = []

    def write_out(t):
        part = pl.ds(pl.multiple_of(offset + t * tile, 128), tile)
        copy = pltpu.make_async_copy(av.at[:, columns(t)], act.at[:, part], sem.at[tiles + t])
        copy.start()
        outs.append(copy)

    def write_tail():
        for pair in range(width // block // 2):
            chip = pair // 2
            base = slot_ref[side, chip * 4 + pair % 2] - holder * block
            if keeps:
                both = jnp.concatenate(
                    [bias_sums[2 * chip + holder], bias_sums[2 * chip + 1 - holder]], axis=0
                )
                both = jnp.concatenate([both, jnp.zeros((16, half - 128), F32)], axis=1)
            else:
                both = jnp.zeros((16, half), F32)
            out[pl.ds(pl.multiple_of(base + 2 * block, 16), 16), :] = both.astype(BF16)

    def wait_weights(t):
        pltpu.make_async_copy(wv.at[:, columns(t)], wv.at[:, columns(t)], sem.at[t]).wait()

    wait_weights(0)
    for m in blocks_of_rows:
        run_linear(0, m)
    cot_copy.wait()
    for t in range(tiles):
        if t + 1 < tiles:
            wait_weights(t + 1)
            for m in blocks_of_rows:
                run_linear(t + 1, m)
        run_gelu(t)
        if t + 1 == tiles and tail:
            write_tail()
        write_out(t)
        run_weight_grad(t)
    for copy in outs:
        copy.wait()


def layer_half(
    start, half, side, tail, tables, token, mixed, mixed_t, bias, cot, alive, pieces, bias_pieces, rows, before, block
):
    node_count, width = mixed.shape
    first = before is None
    tile = min(256, half)
    sub = min(512, node_count)
    groups = width // 128
    out_rows = width + 16 * (width // block // 2) if tail else width
    plan = (
        start,
        half,
        side,
        first,
        tail,
        tail and side == 1,
        pieces[0].ndim == 2,
        [piece.shape[0] for piece in pieces if piece.ndim == 3],
        [piece.shape[0] for piece in bias_pieces],
        pieces[0].shape[1] // rows if pieces[0].ndim == 3 else 0,
        rows,
        tile,
        sub,
        block,
    )
    operands = [*tables, token]
    operands += [held(array, pltpu.VMEM) for array in (mixed, mixed_t)]
    operands += [held(cot, pltpu.HBM), alive]
    operands += [held(array, pltpu.HBM) for array in (*pieces, *bias_pieces)]
    specs = [SMEM] * 4 + [HBM, VMEM, VMEM, HBM, VMEM] + [HBM] * (len(pieces) + len(bias_pieces))
    if not bias_pieces:
        operands.append(bias)
        specs.append(VMEM)
    aliases = {}
    if not first:
        operands += list(before)
        specs += [VMEM, HBM]
        aliases = {len(operands) - 1: 0}
    out_specs = [HBM, VMEM, VMEM, VMEM, VMEM]
    out_shape = [
        pltpu.HBM((node_count, width), BF16),
        pltpu.VMEM((out_rows, half), BF16),
        jax.ShapeDtypeStruct((groups, 8, 128), F32),
        pltpu.VMEM((node_count, half), BF16),
        pltpu.VMEM((width, half), BF16),
    ]
    if bias_pieces:
        out_specs.append(VMEM)
        out_shape.append(jax.ShapeDtypeStruct((groups, 8, 128), F32))
    return pl.pallas_call(
        functools.partial(half_kernel, plan),
        in_specs=specs,
        out_specs=out_specs,
        out_shape=out_shape,
        scratch_shapes=[
            pltpu.VMEM((node_count, half), BF16),
            pltpu.VMEM((node_count, half), BF16),
            pltpu.VMEM((2, node_count, tile), F32),
            pltpu.VMEM((groups, 16, 128), BF16),
            pltpu.SemaphoreType.DMA((2 * (half // tile) + 2,)),
        ],
        input_output_aliases=aliases,
        compiler_params=pltpu.CompilerParams(vmem_limit_bytes=16 * MIB),
        cost_estimate=cost(8),
        name="layer_half",
    )(*operands)


def mixed_grad_kernel(count, scale, *refs):
    grads, weights, (out, token) = refs[:count], refs[count : 2 * count], refs[2 * count :]
    token[...] = jnp.zeros_like(token)
    node_count, width = out.shape
    tile = min(256, width)
    sub = min(512, node_count)
    for d in range(0, width, tile):
        for m in range(0, node_count, sub):
            part = sum(
                small_dot(grad[m : m + sub, :], weight[d : d + tile, :], ((1,), (1,)))
                for grad, weight in zip(grads, weights)
            )
            part = part * jnp.concatenate([scale[m : m + sub, :]] * (tile // 128), axis=1)
            out[m : m + sub, d : d + tile] = part.astype(BF16)


def mixed_grad(scale, grads, weights):
    node_count, width = grads[0].shape[0], weights[0].shape[0]
    return pl.pallas_call(
        functools.partial(mixed_grad_kernel, len(grads)),
        in_specs=[VMEM] * (1 + 2 * len(grads)),
        out_specs=[VMEM, VMEM],
        out_shape=[
            jax.ShapeDtypeStruct((node_count, width), BF16),
            jax.ShapeDtypeStruct((8, 128), F32),
        ],
        compiler_params=pltpu.CompilerParams(vmem_limit_bytes=16 * MIB),
        cost_estimate=cost(10),
        name="mixed_grad",
    )(scale, *[held(array, pltpu.VMEM) for array in (*grads, *weights)])


def rim_grad_kernel(sizes, cnt_t_ref, grad_ref, *outs):
    node_count = grad_ref.shape[0]
    part = small_dot(cnt_t_ref[node_count:, :], grad_ref[...])
    at = 0
    for out, rows in zip(outs, sizes):
        out[...] = part[at : at + rows].astype(BF16)
        at += rows


def rim_grads(cnt_t, grad, sizes):
    micro, table, node_count = cnt_t.shape
    width = grad.shape[1]
    wide = min(512, width)
    return pl.pallas_call(
        functools.partial(rim_grad_kernel, sizes),
        grid=(micro, width // wide),
        in_specs=[
            pl.BlockSpec((None, table, node_count), lambda m, j: (m, 0, 0)),
            pl.BlockSpec((node_count, wide), lambda m, j: (m, j)),
        ],
        out_specs=[pl.BlockSpec((None, rows, wide), lambda m, j: (m, 0, j)) for rows in sizes],
        out_shape=[jax.ShapeDtypeStruct((micro, rows, width), BF16) for rows in sizes],
        compiler_params=pltpu.CompilerParams(vmem_limit_bytes=24 * MIB),
        cost_estimate=cost(3),
        name="rim_grads",
    )(cnt_t, grad)


def own_grad_kernel(cnt_t_ref, grad_ref, out_ref, head_ref):
    part = small_dot(cnt_t_ref[...], grad_ref[...])
    out_ref[...] = part.astype(BF16)
    head_ref[...] = part[: head_ref.shape[0]]


def own_grads(cnt_t, grad, rim_size):
    micro, _, node_count = cnt_t.shape
    width = grad.shape[1]
    wide = min(512, width)
    return pl.pallas_call(
        own_grad_kernel,
        grid=(micro, width // wide),
        in_specs=[
            pl.BlockSpec((None, node_count, node_count), lambda m, j: (m, 0, 0)),
            pl.BlockSpec((node_count, wide), lambda m, j: (m, j)),
        ],
        out_specs=[
            pl.BlockSpec((None, node_count, wide), lambda m, j: (m, 0, j)),
            pl.BlockSpec((None, rim_size, wide), lambda m, j: (m, 0, j)),
        ],
        out_shape=[
            jax.ShapeDtypeStruct((micro, node_count, width), BF16),
            jax.ShapeDtypeStruct((micro, rim_size, width), F32),
        ],
        compiler_params=pltpu.CompilerParams(vmem_limit_bytes=24 * MIB),
        cost_estimate=cost(4),
        name="own_grads",
    )(cnt_t, grad)


class Layout:
    def __init__(self, blks, shards):
        self.blks, self.shards = blks, shards
        self.tuned = shards == 2 and blks == 16
        self.sizes = {"h": blks // 8, "l": 2, "y": 2, "c": 2, "x": shards}

    def number(self, at):
        blk = ((at["h"] * 2 + at["l"]) * 2 + at["y"]) * 2 + at["c"]
        return blk * self.shards + at["x"]

    def place(self, blk, shard):
        return {"h": blk // 8, "l": blk // 4 % 2, "y": blk // 2 % 2, "c": blk % 2, "x": shard}

    def here(self):
        return self.place(lax.axis_index("blk"), lax.axis_index("shard"))

    def spots(self):
        for number in range(self.blks * self.shards):
            yield self.place(number // self.shards, number % self.shards)

    def flip(self, value, axes):
        pairs = []
        for spot in self.spots():
            there = {axis: at ^ (axis in axes[spot["c"]]) for axis, at in spot.items()}
            pairs.append((self.number(spot), self.number(there)))
        return lax.ppermute(value, BOTH, pairs)

    def swap(self, value):
        return self.flip(value, "cc")


def from_shard(value, by):
    count = lax.axis_size("shard")
    return lax.ppermute(value, "shard", [(i, (i + by) % count) for i in range(count)])


def near_swap(value):
    count = lax.axis_size("blk")
    return lax.ppermute(value, "blk", [(i, i ^ 1) for i in range(count)])


def far_swap(value):
    count = lax.axis_size("blk")
    return lax.ppermute(value, "blk", [(i, (i + (1 if i % 2 else -1)) % count) for i in range(count)])


def tie(value, *others):
    return lax.optimization_barrier((value, others))[0]


def gather_step(layout, current, orders, step):
    return [current, layout.flip(current, (orders[0][step], orders[1][step]))]


def reduce_step(layout, parts, orders, step):
    size = parts[0].shape[0] // 2
    total = sum(part[:size].astype(F32) for part in parts).astype(BF16)
    got = layout.flip(total, (orders[0][step], orders[1][step]))
    return [part[size:] for part in parts] + [got]


def gathered_from(layout, order, bases):
    current = [{"c": b} for b in range(bases)]
    for axis in order:
        current = [dict(entry, **{axis: k}) for k in range(layout.sizes[axis]) for entry in current]
    return current


def gathered_numbers(layout, orders, bases, here, swapped):
    core = here["c"] ^ 1 if swapped else here["c"]
    tables = []
    for order in orders:
        entries = gathered_from(layout, order, bases)
        tables.append({axis: np.array([e[axis] for e in entries], np.int32) for axis in "hlycx"})
    back = {axis: jnp.where(core == 0, tables[0][axis], tables[1][axis]) for axis in "hlycx"}
    at = {axis: (here[axis] - back[axis]) % layout.sizes[axis] for axis in "hlyx"}
    at["c"] = core ^ back["c"]
    return layout.number(at)


def slots_of(layout, orders, here, swapped):
    core = here["c"] ^ 1 if swapped else here["c"]
    number = np.arange(layout.blks * layout.shards)
    at = layout.place(number // layout.shards, number % layout.shards)
    results = []
    for order in orders:
        slot = 0
        for axis in order:
            count = layout.sizes[axis]
            ahead = (at[axis] - here[axis]) % count
            slot = slot * count + (ahead - 1) % count
        results.append(slot * 2 + (at["c"] ^ core))
    return jnp.where(core == 0, results[0], results[1]).astype(jnp.int32)


class Flow:
    def __init__(self, tied):
        self.tied, self.values, self.fresh = tied, {}, set()

    def __getitem__(self, name):
        return self.values[name]

    def __setitem__(self, name, value):
        self.values[name] = value
        self.fresh.add(name)

    def seal(self, *names):
        names = names or sorted(self.fresh, key=str)
        if self.tied and names:
            made = lax.optimization_barrier([self.values[name] for name in names])
            self.values.update(zip(names, made))
        self.fresh -= set(names)


def per_device(layout, features, weight, bias, cotangent, neighbours, live_count):
    micro_count, node_count, width = features.shape
    shards = layout.shards
    devices = layout.blks * shards
    rim = node_count // 8
    span = shards * rim
    own_rows = weight.shape[0]
    here = layout.here()
    core = here["c"]
    tuned = layout.tuned and own_rows * shards == 128
    chunks = []
    at = 0
    for share in CHUNKS:
        chunks.append((at, int(width * share)))
        at += int(width * share)
    flow = Flow(tuned)

    def gather(j, step):
        if not tuned:
            return
        order = GATHER_ORDER[j]

        def flip(blocks, at):
            return layout.flip(blocks, (order[0][at], order[1][at]))

        if step < 2:
            both = jnp.concatenate([flow["blocks", j], flip(flow["blocks", j], step)])
            if j == 0 and step == 1:
                count, deep = both.shape[0], 2 * own_rows
                tails = jnp.concatenate([both[k, deep:, :128] for k in range(count)], axis=1)
                tails = jnp.pad(tails, ((0, 0), (0, both.shape[2] - tails.shape[1])))
                both = jnp.concatenate([both[:, :deep].reshape(count * deep, -1), tails])[None]
            flow["blocks", j] = both
        elif step == 2:
            flow["third", j] = flip(flow["blocks", j], 2)
            flow["fourth", j] = flip(flow["blocks", j], 3)
        else:
            flow["last", j] = flip(flow["third", j], 3)

    NAMES = ("blocks", "third", "fourth", "last")

    def swap_pieces(j, *which):
        if tuned:
            for k in which:
                flow["others", j, k] = layout.swap(flow[NAMES[k], j])

    def swap_out(j):
        if tuned:
            flow["parts", j] = [layout.swap(flow["out", j, 0])]

    def reduce(j, step):
        if tuned:
            flow["parts", j] = reduce_step(layout, flow["parts", j], REDUCE_ORDER[j], step)

    def add_and_flip(parts, order, step):
        total = sum(part.astype(F32) for part in parts).astype(BF16)
        return layout.flip(total, (order[0][step], order[1][step]))

    def reduce_first(j, begin, end):
        if tuned:
            parts = [flow["out", j, 1], *flow["parts", j]]
            flow["first", j, begin] = add_and_flip(
                [part[begin:end] for part in parts], REDUCE_ORDER[j], 0
            )

    def reduce_second(j, split):
        if tuned:
            parts = [flow["out", j, 1], *flow["parts", j]]
            size = parts[0].shape[0] // 4
            early = flow["first", j, 0]
            if split < 2 * size:
                late = add_and_flip([part[split : 2 * size] for part in parts], REDUCE_ORDER[j], 0)
            got = add_and_flip(
                [part[2 * size : 3 * size] for part in parts] + [early[:size]], REDUCE_ORDER[j], 1
            )
            flow["parts", j] = [part[3 * size :] for part in parts] + [got]
            if split < 2 * size:
                flow["split", j] = [early[size:], late]
            else:
                flow["split", j] = [early[size : size + size // 2], early[size + size // 2 :]]

    def reduce_third(j):
        if tuned:
            early, late = flow["split", j]
            parts = flow["parts", j]
            size = parts[0].shape[0] // 2
            got = add_and_flip([part[:size] for part in parts] + [early], REDUCE_ORDER[j], 2)
            flow["parts", j] = [part[size:] for part in parts] + [late, got]

    rim_own = features[:, :rim]
    flow["far"] = far_swap(rim_own)
    flow["cross"] = [from_shard(rim_own, shards - k) for k in range(1, shards)]

    if tuned:
        block = rows = own_rows
        numbers = [
            [gathered_numbers(layout, order, 2, here, flag) for flag in (True, False)]
            for order in GATHER_ORDER
        ]
        places = [jnp.stack(pair) * own_rows for pair in numbers]
        numbers = numbers[0][1]
        chip = (numbers // 4 * 2 + numbers % 2)[::2]
        slots = [
            jnp.stack([slots_of(layout, order, here, flag) for flag in (True, False)])
            for order in REDUCE_ORDER
        ]
        slots = [
            slot // 2 * (2 * block + (16 if j + 1 == len(chunks) else 0)) + slot % 2 * block
            for j, slot in enumerate(slots)
        ]
        halves = [
            jnp.concatenate([weight[:, s + h * n // 2 : s + (h + 1) * n // 2] for s, n in chunks], axis=1)
            for h in range(2)
        ]
        lane = jnp.where(
            here["x"] == 0, jnp.pad(bias, (0, 128 - own_rows)), jnp.pad(bias, (128 - own_rows, 0))
        )
        bias_block = jnp.broadcast_to(jnp.pad(lane, (0, width // 2 - 128))[None], (8, width // 2))
        ours = jnp.where(core == 0, halves[0], halves[1])
        theirs = layout.swap(
            jnp.concatenate([jnp.where(core == 0, halves[1], halves[0]), bias_block], axis=0)
        )
        at = 0
        for j, (_, size) in enumerate(chunks):
            cols = slice(at, at + size // 2)
            blocks = [ours[:, cols], theirs[:own_rows, cols]]
            if j == 0:
                blocks += [bias_block[:, cols], theirs[own_rows:, cols]]
            flow["blocks", j] = jnp.concatenate(blocks, axis=0)[None]
            at += size // 2
        flow["bias"] = None
    else:
        block = rows = 64
        places = [jnp.zeros((2, 1), jnp.int32)] * len(chunks)
        chip = jnp.zeros((2,), jnp.int32)
        slots = [
            jnp.broadcast_to(jnp.arange(0, width, block, dtype=jnp.int32), (2, width // block))
        ] * len(chunks)
        theirs = weight
        for j, (start, size) in enumerate(chunks):
            whole = lax.all_gather(weight[:, start : start + size], BOTH, axis=0, tiled=True)
            flow["pieces", j] = [whole]
        bias_full = lax.all_gather(bias, BOTH, axis=0, tiled=True).astype(F32)
        flow["bias"] = jnp.broadcast_to(
            bias_full.reshape(width // 128, 1, 128), (width // 128, 8, 128)
        )
    tables = (places, chip, slots, core.reshape(1))
    tables = jax.tree.map(lambda array: array.astype(jnp.int32), tables)
    neighbours, tables = tie((neighbours, tables), theirs)
    places, chip, slots, core_table = tables

    gather(0, 0)

    table = node_count + (3 * shards - 1) * rim
    shifted = neighbours - node_count
    section = shifted // span
    ahead = (shifted // rim % shards - here["x"]) % shards
    near_section = jnp.where(core == 0, 2, 1)
    base_slot = jnp.where(
        section == 0,
        node_count - rim,
        jnp.where(section == near_section, node_count + span - rim, node_count + 2 * span - rim),
    )
    slot = base_slot + ahead * rim + shifted % rim
    slot = jnp.where((section == 0) & (ahead == 0), shifted % rim, slot)
    codes = jnp.where(neighbours < node_count, neighbours, slot)
    degree = jnp.sum((neighbours >= 0).astype(F32), axis=2)
    alive = (jnp.arange(node_count, dtype=jnp.int32)[None, :] < live_count).astype(F32)
    weighting = alive / (degree + 1.0)
    total_nodes = micro_count * node_count
    flow["alive"] = jnp.broadcast_to(alive.reshape(total_nodes, 1), (total_nodes, 128))
    flow["scale"] = jnp.broadcast_to(weighting.reshape(total_nodes, 1), (total_nodes, 128))
    flow["cnt"], flow["cnt_t"] = count_tables(codes, table)
    flow.seal()

    gather(0, 1)
    far, cross = flow["far"], flow["cross"]
    flow["far_cross_0"] = [from_shard(far[0], shards - k) for k in range(1, shards)]
    flow["far_cross_1"] = far_swap(jnp.concatenate([rows_of[1] for rows_of in cross]))
    flow["near"] = near_swap(jnp.concatenate([rim_own, *cross], axis=1))
    if tuned:
        flow["blocks", 1] = flow["blocks", 1]
    flow.seal()

    gather(0, 2)
    gather(1, 0)
    mixed, mixed_t, flow["token"] = mix(
        flow["cnt"],
        flow["scale"],
        features,
        [
            [*(rows_of[m] for rows_of in cross), flow["near"][m], far[m], *others]
            for m, others in enumerate((flow["far_cross_0"], [flow["far_cross_1"]]))
        ],
    )
    flow.seal()

    gather(0, 3)
    swap_pieces(0, 0, 1, 2)
    gather(1, 1)
    flow.seal()

    cot_rows = cotangent.reshape(total_nodes, width)
    grads, weights = [], []
    flow["before"] = None

    def half_layer(j, side):
        start, size = chunks[j]
        half = size // 2
        if tuned:
            mine = [flow[name, j] for name in NAMES]
            pieces = mine if side else [flow["others", j, k] for k in range(len(mine))]
            bias_pieces = mine if flow["bias"] is None else []
        else:
            pieces, bias_pieces = flow["pieces", j], []
        took = layer_half(
            start,
            half,
            side,
            tuned and j + 1 == len(chunks),
            [places[j], chip, slots[j], core_table],
            flow["token"],
            mixed,
            mixed_t,
            flow["bias"],
            cot_rows,
            flow["alive"],
            pieces,
            bias_pieces,
            rows,
            flow["before"],
            block,
        )
        act, out, bias_sums, grad_part, weight_part = took[:5]
        if len(took) == 6:
            flow["bias"] = took[5]
        flow["before"] = (bias_sums, act)
        grads.append(grad_part)
        weights.append(weight_part)
        flow["out", j, side] = out.reshape(devices // 2, -1, half) if tuned else out

    gather(1, 2)
    swap_pieces(0, 3)
    swap_pieces(1, 0)
    half_layer(0, 0)
    flow.seal()

    gather(1, 3)
    swap_pieces(1, 1, 2)
    swap_out(0)
    half_layer(0, 1)
    flow.seal()

    reduce_first(0, 0, SPLIT_AT[0])
    swap_pieces(1, 3)
    half_layer(1, 0)
    flow.seal()

    reduce_second(0, SPLIT_AT[0])
    swap_out(1)
    half_layer(1, 1)
    flow.seal()

    reduce_first(1, 0, SPLIT_AT[1])
    reduce_third(0)
    sizes = [rim] * (shards - 1) + [span] + [rim] * shards
    grad, flow["after_grad"] = mixed_grad(flow["scale"], grads, weights)
    flow["rims"] = rim_grads(flow["cnt_t"], grad, sizes)
    flow["before_grad"] = flow["cnt_t"]
    flow.seal()

    reduce_second(1, SPLIT_AT[1])
    reduce(0, 3)
    parts = flow["rims"]
    flow["rims"] = parts[: shards - 1], parts[shards:]
    flow["near_back"] = near_swap(parts[shards - 1])
    flow["local"], flow["head"] = own_grads(flow["before_grad"], grad, rim)
    flow.seal()

    reduce_third(1)
    cross, far = flow["rims"]
    near_back = flow["near_back"].astype(F32)

    def toward(m, k):
        return cross[k - 1][m].astype(F32) + near_back[m, k * rim : (k + 1) * rim]

    flow["hop_1"] = far_swap(jnp.concatenate([part[1] for part in far]))
    flow["hop_0"] = [
        from_shard(jnp.concatenate([toward(0, k).astype(BF16), far[k][0]]), k)
        for k in range(1, shards)
    ]
    flow.seal()

    hop_0, hop_1, head = flow["hop_0"], flow["hop_1"].astype(F32), flow["head"]
    back_1 = [
        from_shard((toward(1, k) + hop_1[k * rim : (k + 1) * rim]).astype(BF16), k)
        for k in range(1, shards)
    ]
    far_sum = far[0][0].astype(F32) + sum(both[rim:].astype(F32) for both in hop_0)
    back_0 = far_swap(far_sum.astype(BF16)).astype(F32)
    reduce(1, 3)
    sum_0 = head[0] + near_back[0, :rim] + sum(both[:rim].astype(F32) for both in hop_0) + back_0
    sum_1 = head[1] + near_back[1, :rim] + hop_1[:rim] + sum(both.astype(F32) for both in back_1)
    head = jnp.stack([sum_0, sum_1]).astype(BF16)
    feature_grad = lax.dynamic_update_slice(flow["local"], head, (0, 0, 0))

    weight_grads = []
    for j in range(len(chunks)):
        if tuned:
            both = sum(part[0].astype(F32) for part in flow["parts", j])
            ours, theirs = both[:block], layout.swap(both[block:])
            low_half = jnp.where(core == 0, ours, theirs[:block])
            high_half = jnp.where(core == 0, theirs[:block], ours)
            if j + 1 == len(chunks):
                sums = both[2 * block : 2 * block + 8, :128] + theirs[block + 8 :, :128]
                sums = jnp.sum(sums, axis=0)
                bias_out = jnp.where(here["x"] == 0, sums[:own_rows], sums[128 - own_rows :])
        else:
            send, keep = flow["out", j, 0], flow["out", j, 1]
            low_half, high_half = (
                lax.psum_scatter(
                    jnp.where(core == which, keep, send), BOTH, scatter_dimension=0, tiled=True
                ).astype(F32)
                for which in (0, 1)
            )
        weight_grads += [low_half, high_half]
    bias_sums, act = flow["before"]
    if not tuned:
        bias_sum = jnp.sum(bias_sums, axis=1).reshape(width)
        bias_out = lax.psum_scatter(bias_sum, BOTH, scatter_dimension=0, tiled=True)

    return (
        act.reshape(features.shape),
        feature_grad,
        jnp.concatenate(weight_grads, axis=1),
        bias_out,
    )


def solution(mesh):
    layout = Layout(mesh.shape["blk"], mesh.shape["shard"])
    rows = P(None, BOTH, None)
    return jax.shard_map(
        functools.partial(per_device, layout),
        mesh=mesh,
        in_specs=(rows, P(BOTH, None), P(BOTH), rows, rows, P(None, BOTH)),
        out_specs=(rows, rows, P(BOTH, None), P(BOTH)),
        check_vma=False,
    )
```
